32 devices in a mesh: grp: 16 (over z, y, x), mem: 2 (over core).
Axes of the slice: x: 2, y: 2, z: 4, core: 2. Of those that a mesh axis runs over, the one named last changes fastest.
Arguments:
- raw_traces: float32 [256, 6030], P(('grp', 'mem')), may hold values from -6 to 6
Outputs:
- correlations: bfloat16 [256, 32, 401], P(('grp', 'mem'))
The draws below stay inside these ranges and needn't reach their ends.
All inputs are finite; a program needn't handle non-finite values.
Results may differ from the reference program's by a relative error of at most 0.0063.
Values may be sent and summed in bfloat16 or wider, within the bound.
A program may use at most 64 MiB of HBM per device.

```python
import math
import jax
import jax.numpy as jnp
from jax import lax

CH_DEV = 8
WINDOWS = 2
WLEN = 1500
NFREQ = 384
TAPS = 32
MAXLAG = 200
LAGS = 401
RAWLEN = 6030
CHANNELS = 256


def steps_of(key, shape, cuts, least, largest):
    loudness, own = 1.0, jax.random.fold_in(key, 6)
    for dim, parts in cuts:
        steps = jnp.exp(jax.random.uniform(jax.random.fold_in(own, dim), (parts,), jnp.float32, least / len(cuts), largest / len(cuts)))
        loudness = loudness * jnp.repeat(steps, shape[dim] // parts).reshape([-1 if axis == dim else 1 for axis in range(len(shape))])
    return loudness


def normal_values(key, shape, spread, reach, pieces=(), held_as=jnp.bfloat16):
    entries = jax.random.normal(key, shape, jnp.float32) * spread
    if len(pieces) > 0:
        entries = steps_of(key, shape, pieces, -0.22, 0.18) * entries
    return jnp.clip(entries, min=-reach, max=reach).astype(held_as)


def setup_inputs(seed: int = 0) -> dict:
    seeds = jax.random.split(jax.random.key(seed), 2)
    return {
        "raw_traces": normal_values(seeds[0], (CHANNELS, RAWLEN), 1.0, 6.0, ((0, 32),), jnp.float32),
    }


def lowpass(taps):
    k = jnp.arange(taps).astype(jnp.float32)
    centre = (taps - 1) / 2.0
    window = 0.5 - 0.5 * jnp.cos(2.0 * math.pi * (k + 0.5) / taps)
    return 0.5 * jnp.sinc((k - centre) * 0.5) * window

def forward_table():
    times = jnp.arange(WLEN).astype(jnp.int32)
    bins = jnp.arange(1, NFREQ + 1).astype(jnp.int32)
    phase = times[:, None] * bins[None, :] % WLEN
    angle = 2.0 * math.pi * phase.astype(jnp.float32) / WLEN
    return jnp.concatenate([jnp.cos(angle), -jnp.sin(angle)], axis=1)

def inverse_table():
    bins = jnp.arange(1, NFREQ + 1).astype(jnp.int32)
    shifts = jnp.arange(LAGS).astype(jnp.int32) - MAXLAG
    phase = jnp.mod(bins[:, None] * shifts[None, :], WLEN)
    angle = 2.0 * math.pi * phase.astype(jnp.float32) / WLEN
    return jnp.concatenate([jnp.cos(angle), -jnp.sin(angle)], axis=0).astype(jnp.bfloat16)

def whiten(raw_traces):
    count = raw_traces.shape[0]
    total = WINDOWS * WLEN
    filt = lowpass(TAPS)
    decimated = jnp.zeros((count, total), jnp.float32)
    for k in range(TAPS):
        piece = lax.slice(raw_traces, (0, k), (count, k + 2 * total - 1), (1, 2))
        decimated = decimated + filt[k] * piece
    frames = decimated.reshape(count * WINDOWS, WLEN)
    spec = jnp.dot(frames, forward_table(), precision=lax.Precision.HIGHEST, preferred_element_type=jnp.float32)
    spec_re = spec[:, :NFREQ]
    spec_im = spec[:, NFREQ:]
    power = spec_re * spec_re + spec_im * spec_im
    level = 0.01 * lax.optimization_barrier(jnp.mean(power, axis=1, keepdims=True))
    factor = 1.0 / jnp.sqrt(power + level + 1e-06)
    white = jnp.concatenate([spec_re * factor, spec_im * factor], axis=1)
    return white.astype(jnp.bfloat16).reshape(count, WINDOWS, 2 * NFREQ)

def reference(raw_traces):
    white = whiten(raw_traces)
    sources = white[::CH_DEV]
    recv = white.astype(jnp.float32)
    recv_re = recv[:, :, :NFREQ]
    recv_im = recv[:, :, NFREQ:]
    table = inverse_table().astype(jnp.float32)
    scale = 1.0 / math.sqrt(WINDOWS * NFREQ)

    def one_source(source):
        src = source.astype(jnp.float32)
        src_re = src[None, :, :NFREQ]
        src_im = src[None, :, NFREQ:]
        cross_re = lax.optimization_barrier(jnp.sum(recv_re * src_re + recv_im * src_im, axis=1))
        cross_im = lax.optimization_barrier(jnp.sum(recv_im * src_re - recv_re * src_im, axis=1))
        cross = jnp.concatenate([cross_re, cross_im], axis=1).astype(jnp.bfloat16).astype(jnp.float32)
        corr = jnp.dot(cross, table, preferred_element_type=jnp.float32) * scale
        return corr.astype(jnp.bfloat16)
    stacked = lax.map(one_source, sources)
    return jnp.transpose(stacked, (1, 0, 2))
```

```python
import functools
import math

import jax
import jax.numpy as jnp
import numpy as np
from jax import lax
from jax.experimental import pallas as pl
from jax.experimental.pallas import tpu as pltpu
from jax.sharding import PartitionSpec as P

WINDOWS = 2
WLEN = 1500
NFREQ = 384
TAPS = 32
MAXLAG = 200
LANES = 128
BLOCKS = -(-WLEN // LANES)
REACH = 3 * LANES
SPAN = 2 * LANES * (BLOCKS - 1) + REACH
MESH = pl.DeviceIdType.MESH


def filter_table():
    k = np.arange(TAPS)
    window = 0.5 - 0.5 * np.cos(2.0 * np.pi * (k + 0.5) / TAPS)
    taps = 0.5 * np.sinc((k - (TAPS - 1) / 2.0) * 0.5) * window
    table = np.zeros((REACH, LANES))
    for n in range(LANES):
        table[2 * n : 2 * n + TAPS, n] = taps
    return table.astype(np.float32)


def forward_table():
    phase = np.arange(WLEN)[:, None] * np.arange(1, NFREQ + 1)[None, :] % WLEN
    angle = 2.0 * np.pi * phase / WLEN
    table = np.zeros((BLOCKS * LANES, 2 * NFREQ))
    table[:WLEN] = np.concatenate([np.cos(angle), -np.sin(angle)], axis=1)
    high = table.astype(jnp.bfloat16)
    return np.stack([high, (table - high.astype(np.float64)).astype(jnp.bfloat16)])


def inverse_table():
    shifts = np.arange(2 * MAXLAG + 1) - MAXLAG
    phase = np.mod(np.arange(1, NFREQ + 1)[:, None] * shifts[None, :], WLEN)
    angle = 2.0 * np.pi * phase / WLEN
    return np.concatenate([np.cos(angle), -np.sin(angle)], axis=0).astype(jnp.bfloat16)


def kernel(groups, members, raw_ref, filt_ref, fwd_ref, inv_ref, out_ref,
           padded, blocks, gathered, cross, send_sem, recv_sem):
    count = groups * members
    grp, mem = lax.axis_index("grp"), lax.axis_index("mem")
    me = grp * members + mem
    channels, length = raw_ref.shape
    lags = inv_ref.shape[1]

    barrier = pltpu.get_barrier_semaphore()

    def greet(step, carry):
        peer = lax.rem(me + step, count)
        pl.semaphore_signal(barrier, inc=1, device_id=(peer // members, lax.rem(peer, members)),
                            device_id_type=MESH)
        return carry

    lax.fori_loop(1, count, greet, 0)

    whole = length // LANES * LANES
    padded[:, whole:] = jnp.zeros((channels, padded.shape[1] - whole), jnp.float32)
    padded[:, :length] = raw_ref[...]
    for w in range(WINDOWS):
        start = 2 * WLEN * w
        base = start // LANES * LANES
        if start == base:
            piece = padded[:, start : start + SPAN]
        else:
            width = SPAN + LANES
            piece = pltpu.roll(padded[:, base : base + width], width - (start - base), 1)
        for b in range(BLOCKS):
            row = (w * BLOCKS + b) * channels
            blocks[row : row + channels, :] = piece[:, 2 * LANES * b : 2 * LANES * b + REACH]
    decimated = jnp.dot(blocks[...], filt_ref[...], precision=lax.Precision.HIGHEST,
                        preferred_element_type=jnp.float32)
    frames = jnp.concatenate(
        [
            jnp.concatenate(
                [
                    decimated[(w * BLOCKS + b) * channels : (w * BLOCKS + b + 1) * channels, :]
                    for b in range(BLOCKS)
                ],
                axis=1,
            )
            for w in range(WINDOWS)
        ],
        axis=0,
    )
    rows = WINDOWS * channels
    high = frames.astype(jnp.bfloat16)
    low = (frames - high.astype(jnp.float32)).astype(jnp.bfloat16)
    parts = jnp.dot(jnp.concatenate([high, low], axis=0), fwd_ref[0],
                    preferred_element_type=jnp.float32)
    spec = parts[:rows] + parts[rows:]
    spec = spec + jnp.dot(high, fwd_ref[1], preferred_element_type=jnp.float32)
    spec_re, spec_im = spec[:, :NFREQ], spec[:, NFREQ:]
    power = spec_re * spec_re + spec_im * spec_im
    level = 0.01 * jnp.mean(power, axis=1, keepdims=True)
    factor = 1.0 / jnp.sqrt(power + level + 1e-06)
    white = jnp.concatenate([spec_re * factor, spec_im * factor], axis=1)
    own = white.astype(jnp.bfloat16).astype(jnp.float32)
    gathered[me] = jnp.concatenate(
        [own[w * channels : w * channels + 1] for w in range(WINDOWS)], axis=0
    ).astype(jnp.bfloat16)

    pl.semaphore_wait(barrier, count - 1)

    def send(step, carry):
        peer = lax.rem(me + step, count)
        pltpu.make_async_remote_copy(
            src_ref=gathered.at[me],
            dst_ref=gathered.at[me],
            send_sem=send_sem,
            recv_sem=recv_sem,
            device_id=(peer // members, lax.rem(peer, members)),
            device_id_type=MESH,
        ).start()
        return carry

    lax.fori_loop(1, count, send, 0)
    others = gathered.at[pl.ds(0, count - 1)]
    pltpu.make_async_copy(others, others, recv_sem).wait()

    panel = min(count, 32)
    size = panel * channels
    to = lax.broadcasted_iota(jnp.int32, (size, size), 0)
    at = lax.broadcasted_iota(jnp.int32, (size, size), 1)
    order = (lax.rem(to, panel) * channels + to // panel == at).astype(jnp.float32).astype(jnp.bfloat16)
    scale = 1.0 / math.sqrt(WINDOWS * NFREQ)

    def work(index, carry):
        for j in range(panel):
            source = gathered[index * panel + j].astype(jnp.float32)
            cross_re = jnp.zeros((channels, NFREQ), jnp.float32)
            cross_im = jnp.zeros((channels, NFREQ), jnp.float32)
            for w in range(WINDOWS):
                a_re = own[w * channels : (w + 1) * channels, :NFREQ]
                a_im = own[w * channels : (w + 1) * channels, NFREQ:]
                b_re = source[w : w + 1, :NFREQ]
                b_im = source[w : w + 1, NFREQ:]
                cross_re = cross_re + (a_re * b_re + a_im * b_im)
                cross_im = cross_im + (a_im * b_re - a_re * b_im)
            cross[j * channels : (j + 1) * channels, :NFREQ] = cross_re
            cross[j * channels : (j + 1) * channels, NFREQ:] = cross_im
        turned = jnp.dot(order, cross[...].astype(jnp.bfloat16),
                         preferred_element_type=jnp.float32).astype(jnp.bfloat16)
        corr = jnp.dot(turned, inv_ref[...], preferred_element_type=jnp.float32) * scale
        corr = corr.astype(jnp.bfloat16)
        for c in range(channels):
            out_ref[c, pl.ds(pl.multiple_of(index * panel, panel), panel), :] = corr[c * panel : (c + 1) * panel]
        return carry

    if count == panel:
        work(0, 0)
    else:
        lax.fori_loop(0, count // panel, work, 0)
    pltpu.make_async_copy(others, others, send_sem).wait()


def solution(mesh):
    groups, members = mesh.shape["grp"], mesh.shape["mem"]
    count = groups * members
    filt, fwd, inv = filter_table(), forward_table(), inverse_table()

    def on_device(raw_traces):
        channels, length = raw_traces.shape
        start = 2 * WLEN * (WINDOWS - 1) // LANES * LANES
        return pl.pallas_call(
            functools.partial(kernel, groups, members),
            out_shape=jax.ShapeDtypeStruct((channels, count, inv.shape[1]), jnp.bfloat16),
            in_specs=[pl.BlockSpec(memory_space=pltpu.VMEM)] * 4,
            out_specs=pl.BlockSpec(memory_space=pltpu.VMEM),
            scratch_shapes=[
                pltpu.VMEM((channels, start + SPAN + LANES), jnp.float32),
                pltpu.VMEM((WINDOWS * BLOCKS * channels, REACH), jnp.float32),
                pltpu.VMEM((count, WINDOWS, 2 * NFREQ), jnp.bfloat16),
                pltpu.VMEM((min(count, 32) * channels, 2 * NFREQ), jnp.float32),
                pltpu.SemaphoreType.DMA,
                pltpu.SemaphoreType.DMA,
            ],
            compiler_params=pltpu.CompilerParams(
                collective_id=0, has_side_effects=True, vmem_limit_bytes=48 * 1024 * 1024
            ),
        )(raw_traces, jnp.asarray(filt), jnp.asarray(fwd), jnp.asarray(inv))

    return jax.shard_map(
        on_device,
        mesh=mesh,
        in_specs=(P(("grp", "mem"), None),),
        out_specs=P(("grp", "mem"), None, None),
        check_vma=False,
    )
```

```python
import functools
import math

import jax
import jax.numpy as jnp
import numpy as np
from jax import lax
from jax.experimental import pallas as pl
from jax.experimental.pallas import tpu as pltpu
from jax.sharding import PartitionSpec as P

WINDOWS = 2
WLEN = 1500
NFREQ = 384
TAPS = 32
MAXLAG = 200
LANES = 128
BLOCKS = -(-WLEN // LANES)
REACH = 3 * LANES
SPAN = 2 * LANES * (BLOCKS - 1) + REACH
VMEM_LIMIT = 48 * 1024 * 1024
MESH = pl.DeviceIdType.MESH


def halves(table):
    high = table.astype(jnp.bfloat16)
    return np.stack([high, (table - high.astype(np.float64)).astype(jnp.bfloat16)])


def filter_table():
    k = np.arange(TAPS)
    window = 0.5 - 0.5 * np.cos(2.0 * np.pi * (k + 0.5) / TAPS)
    taps = 0.5 * np.sinc((k - (TAPS - 1) / 2.0) * 0.5) * window
    table = np.zeros((REACH, LANES))
    for n in range(LANES):
        table[2 * n : 2 * n + TAPS, n] = taps
    return halves(table)


def wave_table(times):
    phase = times[:, None] * np.arange(1, NFREQ + 1)[None, :] % WLEN
    angle = 2.0 * np.pi * phase / WLEN
    return np.concatenate([np.cos(angle), -np.sin(angle)], axis=1)


def inverse_table():
    shifts = np.arange(2 * MAXLAG + 1) - MAXLAG
    phase = np.mod(np.arange(1, NFREQ + 1)[:, None] * shifts[None, :], WLEN)
    angle = 2.0 * np.pi * phase / WLEN
    return np.concatenate([np.cos(angle), -np.sin(angle)], axis=0).astype(jnp.bfloat16)


def split_dot(left, right):
    high = left.astype(jnp.bfloat16)
    low = (left - high.astype(jnp.float32)).astype(jnp.bfloat16)
    return jnp.dot(jnp.concatenate([high, low, high], axis=1),
                   jnp.concatenate([right[0], right[0], right[1]], axis=0),
                   preferred_element_type=jnp.float32)


def kernel(groups, members, *refs):
    operands, out_ref = refs[:5], refs[5]
    held, (padded, blocks, gathered, cross, load_sem, send_sem, recv_sem) = refs[6:11], refs[11:]
    raw_ref, filt_ref, near_ref, far_ref, inv_ref = held
    count = groups * members
    grp, mem = lax.axis_index("grp"), lax.axis_index("mem")
    me = grp * members + mem
    channels, length = raw_ref.shape

    loads = [pltpu.make_async_copy(operands[i], held[i], load_sem.at[i]) for i in range(5)]
    for load in loads:
        load.start()
    barrier = pltpu.get_barrier_semaphore()

    def greet(step, carry):
        peer = lax.rem(me + step, count)
        pl.semaphore_signal(barrier, inc=1, device_id=(peer // members, lax.rem(peer, members)),
                            device_id_type=MESH)
        return carry

    lax.fori_loop(1, count, greet, 0)

    whole = length // LANES * LANES
    padded[:, whole:] = jnp.zeros((channels, padded.shape[1] - whole), jnp.float32)
    loads[0].wait()
    padded[:, :length] = raw_ref[...]
    for w in range(WINDOWS):
        start = 2 * WLEN * w
        base = start // LANES * LANES
        if start == base:
            piece = padded[:, start : start + SPAN]
        else:
            width = SPAN + LANES
            piece = pltpu.roll(padded[:, base : base + width], width - (start - base), 1)
        for b in range(BLOCKS):
            row = (w * BLOCKS + b) * channels
            blocks[row : row + channels, :] = piece[:, 2 * LANES * b : 2 * LANES * b + REACH]
    loads[1].wait()
    decimated = split_dot(blocks[...], filt_ref)
    inside = lax.broadcasted_iota(jnp.int32, (channels, LANES), 1) < WLEN - (BLOCKS - 1) * LANES
    kept = []
    for w in range(WINDOWS):
        first = w * BLOCKS * channels
        last = first + (BLOCKS - 1) * channels
        kept += [decimated[first:last], jnp.where(inside, decimated[last : last + channels], 0.0)]
    decimated = jnp.concatenate(kept, axis=0)

    loads[2].wait()
    parts = split_dot(decimated, near_ref)
    loads[3].wait()
    sums_re, sums_im = [], []
    for w in range(WINDOWS):
        sum_re = sum_im = None
        for b in range(BLOCKS):
            row = (w * BLOCKS + b) * channels
            part_re = parts[row : row + channels, :NFREQ]
            part_im = parts[row : row + channels, NFREQ:]
            turn_re = far_ref[b : b + 1, :NFREQ]
            turn_im = far_ref[b : b + 1, NFREQ:]
            if b == 0:
                sum_re, sum_im = part_re, part_im
            else:
                sum_re = sum_re + (part_re * turn_re - part_im * turn_im)
                sum_im = sum_im + (part_re * turn_im + part_im * turn_re)
        sums_re.append(sum_re)
        sums_im.append(sum_im)
    spec_re = jnp.concatenate(sums_re, axis=0)
    spec_im = jnp.concatenate(sums_im, axis=0)
    power = spec_re * spec_re + spec_im * spec_im
    level = 0.01 * jnp.mean(power, axis=1, keepdims=True)
    factor = 1.0 / jnp.sqrt(power + level + 1e-06)
    white = jnp.concatenate([spec_re * factor, spec_im * factor], axis=1)
    own = white.astype(jnp.bfloat16).astype(jnp.float32)
    gathered[me] = jnp.concatenate(
        [own[w * channels : w * channels + 1] for w in range(WINDOWS)], axis=0
    ).astype(jnp.bfloat16)

    pl.semaphore_wait(barrier, count - 1)

    def send(step, carry):
        peer = lax.rem(me + step, count)
        pltpu.make_async_remote_copy(
            src_ref=gathered.at[me],
            dst_ref=gathered.at[me],
            send_sem=send_sem,
            recv_sem=recv_sem,
            device_id=(peer // members, lax.rem(peer, members)),
            device_id_type=MESH,
        ).start()
        return carry

    lax.fori_loop(1, count, send, 0)
    others = gathered.at[pl.ds(0, count - 1)]
    pltpu.make_async_copy(others, others, recv_sem).wait()

    panel = min(count, 32)
    size = panel * channels
    to = lax.broadcasted_iota(jnp.int32, (size, size), 0)
    at = lax.broadcasted_iota(jnp.int32, (size, size), 1)
    order = (lax.rem(to, panel) * channels + to // panel == at).astype(jnp.float32).astype(jnp.bfloat16)
    scale = 1.0 / math.sqrt(WINDOWS * NFREQ)

    loads[4].wait()

    def work(index, carry):
        for j in range(panel):
            source = gathered[index * panel + j].astype(jnp.float32)
            cross_re = jnp.zeros((channels, NFREQ), jnp.float32)
            cross_im = jnp.zeros((channels, NFREQ), jnp.float32)
            for w in range(WINDOWS):
                a_re = own[w * channels : (w + 1) * channels, :NFREQ]
                a_im = own[w * channels : (w + 1) * channels, NFREQ:]
                b_re = source[w : w + 1, :NFREQ]
                b_im = source[w : w + 1, NFREQ:]
                cross_re = cross_re + (a_re * b_re + a_im * b_im)
                cross_im = cross_im + (a_im * b_re - a_re * b_im)
            cross[j * channels : (j + 1) * channels, :NFREQ] = cross_re
            cross[j * channels : (j + 1) * channels, NFREQ:] = cross_im
        turned = jnp.dot(order, cross[...].astype(jnp.bfloat16),
                         preferred_element_type=jnp.float32).astype(jnp.bfloat16)
        corr = jnp.dot(turned, inv_ref[...], preferred_element_type=jnp.float32) * scale
        corr = corr.astype(jnp.bfloat16)
        for c in range(channels):
            out_ref[c, pl.ds(pl.multiple_of(index * panel, panel), panel), :] = corr[c * panel : (c + 1) * panel]
        return carry

    if count == panel:
        work(0, 0)
    else:
        lax.fori_loop(0, count // panel, work, 0)
    pltpu.make_async_copy(others, others, send_sem).wait()


def solution(mesh):
    groups, members = mesh.shape["grp"], mesh.shape["mem"]
    count = groups * members
    tables = [
        filter_table(),
        halves(wave_table(np.arange(LANES))),
        wave_table(LANES * np.arange(BLOCKS)).astype(np.float32),
        inverse_table(),
    ]

    def on_device(raw_traces):
        channels, length = raw_traces.shape
        start = 2 * WLEN * (WINDOWS - 1) // LANES * LANES
        operands = [raw_traces] + [jnp.asarray(table) for table in tables]
        return pl.pallas_call(
            functools.partial(kernel, groups, members),
            out_shape=jax.ShapeDtypeStruct((channels, count, 2 * MAXLAG + 1), jnp.bfloat16),
            in_specs=[pl.BlockSpec(memory_space=pltpu.HBM)] * len(operands),
            out_specs=pl.BlockSpec(memory_space=pltpu.VMEM),
            scratch_shapes=[pltpu.VMEM(x.shape, x.dtype) for x in operands]
            + [
                pltpu.VMEM((channels, start + SPAN + LANES), jnp.float32),
                pltpu.VMEM((WINDOWS * BLOCKS * channels, REACH), jnp.float32),
                pltpu.VMEM((count, WINDOWS, 2 * NFREQ), jnp.bfloat16),
                pltpu.VMEM((min(count, 32) * channels, 2 * NFREQ), jnp.float32),
                pltpu.SemaphoreType.DMA((len(operands),)),
                pltpu.SemaphoreType.DMA,
                pltpu.SemaphoreType.DMA,
            ],
            compiler_params=pltpu.CompilerParams(
                collective_id=0, has_side_effects=True, vmem_limit_bytes=VMEM_LIMIT
            ),
        )(*operands)

    return jax.shard_map(
        on_device,
        mesh=mesh,
        in_specs=(P(("grp", "mem"), None),),
        out_specs=P(("grp", "mem"), None, None),
        check_vma=False,
    )
```

```python
import functools
import math

import jax
import jax.numpy as jnp
import numpy as np
from jax import lax
from jax.experimental import pallas as pl
from jax.experimental.pallas import tpu as pltpu
from jax.sharding import PartitionSpec as P

WINDOWS = 2
WLEN = 1500
NFREQ = 384
TAPS = 32
MAXLAG = 200
LANES = 128
BLOCKS = -(-WLEN // LANES)
REACH = 3 * LANES
SPAN = 2 * LANES * (BLOCKS - 1) + REACH
VMEM_LIMIT = 48 * 1024 * 1024
LOGICAL = pl.DeviceIdType.LOGICAL


def halves(table):
    high = table.astype(jnp.bfloat16)
    return np.stack([high, (table - high.astype(np.float64)).astype(jnp.bfloat16)])


def filter_table():
    k = np.arange(TAPS)
    window = 0.5 - 0.5 * np.cos(2.0 * np.pi * (k + 0.5) / TAPS)
    taps = 0.5 * np.sinc((k - (TAPS - 1) / 2.0) * 0.5) * window
    table = np.zeros((REACH, LANES))
    for n in range(LANES):
        table[2 * n : 2 * n + TAPS, n] = taps
    return halves(table)


def wave_table(times):
    phase = times[:, None] * np.arange(1, NFREQ + 1)[None, :] % WLEN
    angle = 2.0 * np.pi * phase / WLEN
    return np.concatenate([np.cos(angle), -np.sin(angle)], axis=1)


def inverse_table():
    shifts = np.arange(2 * MAXLAG + 1) - MAXLAG
    phase = np.mod(np.arange(1, NFREQ + 1)[:, None] * shifts[None, :], WLEN)
    angle = 2.0 * np.pi * phase / WLEN
    return np.concatenate([np.cos(angle), -np.sin(angle)], axis=0).astype(jnp.bfloat16)


def split_dot(left, right):
    high = left.astype(jnp.bfloat16)
    low = (left - high.astype(jnp.float32)).astype(jnp.bfloat16)
    return jnp.dot(jnp.concatenate([high, low, high], axis=1),
                   jnp.concatenate([right[0], right[0], right[1]], axis=0),
                   preferred_element_type=jnp.float32)


def whiten(spec_re, spec_im):
    power = spec_re * spec_re + spec_im * spec_im
    level = 0.01 * jnp.mean(power, axis=1, keepdims=True)
    factor = 1.0 / jnp.sqrt(power + level + 1e-06)
    return jnp.concatenate([spec_re * factor, spec_im * factor], axis=1).astype(jnp.bfloat16)


def kernel(groups, members, *refs):
    operands, out_ref = refs[:5], refs[5]
    held, (padded, lead, blocks, gathered, cross, load_sem, send_sem, recv_sem) = refs[6:11], refs[11:]
    raw_ref, filt_ref, near_ref, far_ref, inv_ref = held
    count = groups * members
    grp, mem = lax.axis_index("grp"), lax.axis_index("mem")
    me = grp * members + mem
    channels, length = raw_ref.shape

    loads = [pltpu.make_async_copy(operands[i], held[i], load_sem.at[i]) for i in range(5)]
    for load in loads:
        load.start()
    barrier = pltpu.get_barrier_semaphore()

    def peer_of(step):
        peer = me + step
        return jnp.where(peer >= count, peer - count, peer)

    def greet(step, carry):
        pl.semaphore_signal(barrier, inc=1, device_id=peer_of(step), device_id_type=LOGICAL)
        return carry

    lax.fori_loop(1, count, greet, 0)

    whole = length // LANES * LANES
    padded[:, whole:] = jnp.zeros((channels, padded.shape[1] - whole), jnp.float32)
    loads[0].wait()
    padded[:, :length] = raw_ref[...]
    for w in range(WINDOWS):
        start = 2 * WLEN * w
        base = start // LANES * LANES
        if start == base:
            piece = padded[:, start : start + SPAN]
        else:
            width = SPAN + LANES
            piece = pltpu.roll(padded[:, base : base + width], width - (start - base), 1)
        for b in range(BLOCKS):
            row = (w * BLOCKS + b) * channels
            block = piece[:, 2 * LANES * b : 2 * LANES * b + REACH]
            blocks[row : row + channels, :] = block
            lead[w * BLOCKS + b : w * BLOCKS + b + 1, :] = block[:1]

    loads[1].wait()
    first = split_dot(lead[...], filt_ref)
    row = lax.broadcasted_iota(jnp.int32, first.shape, 0)
    beyond = lax.broadcasted_iota(jnp.int32, first.shape, 1) >= WLEN - (BLOCKS - 1) * LANES
    first = jnp.where((lax.rem(row, BLOCKS) == BLOCKS - 1) & beyond, 0.0, first)
    loads[2].wait()
    parts = split_dot(first, near_ref)
    loads[3].wait()
    part_re, part_im = parts[:, :NFREQ], parts[:, NFREQ:]
    turn_re, turn_im = far_ref[:, :NFREQ], far_ref[:, NFREQ:]
    window = lax.broadcasted_iota(jnp.int32, part_re.shape, 0) // BLOCKS
    sums = []
    for turned in (part_re * turn_re - part_im * turn_im, part_re * turn_im + part_im * turn_re):
        sums.append(jnp.concatenate(
            [
                jnp.sum(jnp.where(window == w, turned, 0.0), axis=0, keepdims=True)
                for w in range(WINDOWS)
            ],
            axis=0,
        ))
    gathered[me] = whiten(*sums)

    pl.semaphore_wait(barrier, count - 1)

    def send(step, carry):
        pltpu.make_async_remote_copy(
            src_ref=gathered.at[me],
            dst_ref=gathered.at[me],
            send_sem=send_sem,
            recv_sem=recv_sem,
            device_id=peer_of(step),
            device_id_type=LOGICAL,
        ).start()
        return carry

    lax.fori_loop(1, count, send, 0)

    decimated = split_dot(blocks[...], filt_ref)
    inside = lax.broadcasted_iota(jnp.int32, (channels, LANES), 1) < WLEN - (BLOCKS - 1) * LANES
    kept = []
    for w in range(WINDOWS):
        first = w * BLOCKS * channels
        last = first + (BLOCKS - 1) * channels
        kept += [decimated[first:last], jnp.where(inside, decimated[last : last + channels], 0.0)]
    decimated = jnp.concatenate(kept, axis=0)

    parts = split_dot(decimated, near_ref)
    sums_re, sums_im = [], []
    for w in range(WINDOWS):
        sum_re = sum_im = None
        for b in range(BLOCKS):
            row = (w * BLOCKS + b) * channels
            part_re = parts[row : row + channels, :NFREQ]
            part_im = parts[row : row + channels, NFREQ:]
            turn_re = far_ref[b : b + 1, :NFREQ]
            turn_im = far_ref[b : b + 1, NFREQ:]
            if b == 0:
                sum_re, sum_im = part_re, part_im
            else:
                sum_re = sum_re + (part_re * turn_re - part_im * turn_im)
                sum_im = sum_im + (part_re * turn_im + part_im * turn_re)
        sums_re.append(sum_re)
        sums_im.append(sum_im)
    spec_re = jnp.concatenate(sums_re, axis=0)
    spec_im = jnp.concatenate(sums_im, axis=0)
    own = whiten(spec_re, spec_im).astype(jnp.float32)

    others = gathered.at[pl.ds(0, count - 1)]

    panel = min(count, 32)
    size = panel * channels
    to = lax.broadcasted_iota(jnp.int32, (size, size), 0)
    at = lax.broadcasted_iota(jnp.int32, (size, size), 1)
    order = (lax.rem(to, panel) * channels + to // panel == at).astype(jnp.float32).astype(jnp.bfloat16)
    scale = 1.0 / math.sqrt(WINDOWS * NFREQ)

    loads[4].wait()
    pltpu.make_async_copy(others, others, recv_sem).wait()

    def work(index, carry):
        for j in range(panel):
            source = gathered[index * panel + j].astype(jnp.float32)
            cross_re = jnp.zeros((channels, NFREQ), jnp.float32)
            cross_im = jnp.zeros((channels, NFREQ), jnp.float32)
            for w in range(WINDOWS):
                a_re = own[w * channels : (w + 1) * channels, :NFREQ]
                a_im = own[w * channels : (w + 1) * channels, NFREQ:]
                b_re = source[w : w + 1, :NFREQ]
                b_im = source[w : w + 1, NFREQ:]
                cross_re = cross_re + (a_re * b_re + a_im * b_im)
                cross_im = cross_im + (a_im * b_re - a_re * b_im)
            cross[j * channels : (j + 1) * channels, :NFREQ] = cross_re
            cross[j * channels : (j + 1) * channels, NFREQ:] = cross_im
        turned = jnp.dot(order, cross[...].astype(jnp.bfloat16),
                         preferred_element_type=jnp.float32).astype(jnp.bfloat16)
        corr = jnp.dot(turned, inv_ref[...], preferred_element_type=jnp.float32) * scale
        corr = corr.astype(jnp.bfloat16)
        for c in range(channels):
            out_ref[c, pl.ds(pl.multiple_of(index * panel, panel), panel), :] = corr[c * panel : (c + 1) * panel]
        return carry

    if count == panel:
        work(0, 0)
    else:
        lax.fori_loop(0, count // panel, work, 0)
    pltpu.make_async_copy(others, others, send_sem).wait()


def solution(mesh):
    groups, members = mesh.shape["grp"], mesh.shape["mem"]
    count = groups * members
    tables = [
        filter_table(),
        halves(wave_table(np.arange(LANES))),
        np.tile(wave_table(LANES * np.arange(BLOCKS)), (WINDOWS, 1)).astype(np.float32),
        inverse_table(),
    ]

    def on_device(raw_traces):
        channels, length = raw_traces.shape
        start = 2 * WLEN * (WINDOWS - 1) // LANES * LANES
        operands = [
            pltpu.with_memory_space_constraint(x, pltpu.HBM)
            for x in [raw_traces] + [jnp.asarray(table) for table in tables]
        ]
        return pl.pallas_call(
            functools.partial(kernel, groups, members),
            out_shape=jax.ShapeDtypeStruct((channels, count, 2 * MAXLAG + 1), jnp.bfloat16),
            in_specs=[pl.BlockSpec(memory_space=pl.ANY)] * len(operands),
            out_specs=pl.BlockSpec(memory_space=pltpu.VMEM),
            scratch_shapes=[pltpu.VMEM(x.shape, x.dtype) for x in operands]
            + [
                pltpu.VMEM((channels, start + SPAN + LANES), jnp.float32),
                pltpu.VMEM((WINDOWS * BLOCKS, REACH), jnp.float32),
                pltpu.VMEM((WINDOWS * BLOCKS * channels, REACH), jnp.float32),
                pltpu.VMEM((count, WINDOWS, 2 * NFREQ), jnp.bfloat16),
                pltpu.VMEM((min(count, 32) * channels, 2 * NFREQ), jnp.float32),
                pltpu.SemaphoreType.DMA((len(operands),)),
                pltpu.SemaphoreType.DMA,
                pltpu.SemaphoreType.DMA,
            ],
            compiler_params=pltpu.CompilerParams(
                collective_id=0, has_side_effects=True, vmem_limit_bytes=VMEM_LIMIT
            ),
        )(*operands)

    return jax.shard_map(
        on_device,
        mesh=mesh,
        in_specs=(P(("grp", "mem"), None),),
        out_specs=P(("grp", "mem"), None, None),
        check_vma=False,
    )
```

```python
import functools
import math

import jax
import jax.numpy as jnp
import numpy as np
from jax import lax
from jax.experimental import pallas as pl
from jax.experimental.pallas import tpu as pltpu
from jax.sharding import PartitionSpec as P

WINDOWS = 2
WLEN = 1500
NFREQ = 384
TAPS = 32
MAXLAG = 200
LANES = 128
BLOCKS = -(-WLEN // LANES)
REACH = 3 * LANES
SPAN = 2 * LANES * (BLOCKS - 1) + REACH
PIECES = 2 * NFREQ // LANES
SLOT = 16
VMEM_LIMIT = 48 * 1024 * 1024
LOGICAL = pl.DeviceIdType.LOGICAL


def halves(table):
    high = table.astype(jnp.bfloat16)
    return np.stack([high, (table - high.astype(np.float64)).astype(jnp.bfloat16)])


def filter_table():
    k = np.arange(TAPS)
    window = 0.5 - 0.5 * np.cos(2.0 * np.pi * (k + 0.5) / TAPS)
    taps = 0.5 * np.sinc((k - (TAPS - 1) / 2.0) * 0.5) * window
    table = np.zeros((REACH, LANES))
    for n in range(LANES):
        table[2 * n : 2 * n + TAPS, n] = taps
    return halves(table)


def wave_table(times):
    phase = times[:, None] * np.arange(1, NFREQ + 1)[None, :] % WLEN
    angle = 2.0 * np.pi * phase / WLEN
    return np.concatenate([np.cos(angle), -np.sin(angle)], axis=1)


def inverse_table():
    shifts = np.arange(2 * MAXLAG + 1) - MAXLAG
    phase = np.mod(np.arange(1, NFREQ + 1)[:, None] * shifts[None, :], WLEN)
    angle = 2.0 * np.pi * phase / WLEN
    return np.concatenate([np.cos(angle), -np.sin(angle)], axis=0).astype(jnp.bfloat16)


def split_dot(left, right):
    high = left.astype(jnp.bfloat16)
    low = (left - high.astype(jnp.float32)).astype(jnp.bfloat16)
    return jnp.dot(jnp.concatenate([high, low, high], axis=1),
                   jnp.concatenate([right[0], right[0], right[1]], axis=0),
                   preferred_element_type=jnp.float32)


def whiten(spec_re, spec_im):
    power = spec_re * spec_re + spec_im * spec_im
    level = 0.01 * jnp.mean(power, axis=1, keepdims=True)
    factor = 1.0 / jnp.sqrt(power + level + 1e-06)
    return jnp.concatenate([spec_re * factor, spec_im * factor], axis=1)


def kernel(groups, members, *refs):
    operands, out_ref = refs[:5], refs[5]
    held, (padded, lead, blocks, gathered, wide, cross, load_sem, send_sem, recv_sem) = refs[6:11], refs[11:]
    raw_ref, filt_ref, near_ref, far_ref, inv_ref = held
    count = groups * members
    grp, mem = lax.axis_index("grp"), lax.axis_index("mem")
    me = grp * members + mem
    channels, length = raw_ref.shape

    loads = [pltpu.make_async_copy(operands[i], held[i], load_sem.at[i]) for i in range(5)]
    for load in loads:
        load.start()
    barrier = pltpu.get_barrier_semaphore()

    def peer_of(step):
        peer = me + jnp.where(step < count // 2, step + count // 2, step - count // 2 + 1)
        return jnp.where(peer >= count, peer - count, peer)

    def greet(step, carry):
        pl.semaphore_signal(barrier, inc=1, device_id=peer_of(step), device_id_type=LOGICAL)
        return carry

    lax.fori_loop(0, count - 1, greet, 0)

    whole = length // LANES * LANES
    padded[:, whole:] = jnp.zeros((channels, padded.shape[1] - whole), jnp.float32)
    loads[0].wait()
    padded[:, :length] = raw_ref[...]
    pieces = []
    for w in range(WINDOWS):
        start = 2 * WLEN * w
        base = start // LANES * LANES
        if start == base:
            piece = padded[:, start : start + SPAN]
        else:
            width = SPAN + LANES
            piece = pltpu.roll(padded[:, base : base + width], width - (start - base), 1)
        pieces.append(piece)
        for b in range(BLOCKS):
            row = w * BLOCKS + b
            lead[row : row + 1, :] = piece[:1, 2 * LANES * b : 2 * LANES * b + REACH]

    loads[1].wait()
    first = split_dot(lead[...], filt_ref)
    row = lax.broadcasted_iota(jnp.int32, first.shape, 0)
    beyond = lax.broadcasted_iota(jnp.int32, first.shape, 1) >= WLEN - (BLOCKS - 1) * LANES
    first = jnp.where((lax.rem(row, BLOCKS) == BLOCKS - 1) & beyond, 0.0, first)
    loads[2].wait()
    parts = split_dot(first, near_ref)
    loads[3].wait()
    part_re, part_im = parts[:, :NFREQ], parts[:, NFREQ:]
    turn_re, turn_im = far_ref[:, :NFREQ], far_ref[:, NFREQ:]
    window = lax.broadcasted_iota(jnp.int32, part_re.shape, 0) // BLOCKS
    sums = []
    for turned in (part_re * turn_re - part_im * turn_im, part_re * turn_im + part_im * turn_re):
        sums.append(jnp.concatenate(
            [
                jnp.sum(jnp.where(window == w, turned, 0.0), axis=0, keepdims=True)
                for w in range(WINDOWS)
            ],
            axis=0,
        ))
    white = whiten(*sums)
    gathered[me] = jnp.concatenate(
        [
            white[w : w + 1, LANES * i : LANES * (i + 1)]
            for w in range(WINDOWS)
            for i in range(PIECES)
        ],
        axis=0,
    ).astype(jnp.bfloat16)

    pl.semaphore_wait(barrier, count - 1)

    def send(step, carry):
        pltpu.make_async_remote_copy(
            src_ref=gathered.at[me],
            dst_ref=gathered.at[me],
            send_sem=send_sem,
            recv_sem=recv_sem,
            device_id=peer_of(step),
            device_id_type=LOGICAL,
        ).start()
        return carry

    lax.fori_loop(0, count - 1, send, 0)

    for w in range(WINDOWS):
        for b in range(BLOCKS):
            row = (w * BLOCKS + b) * channels
            blocks[row : row + channels, :] = pieces[w][:, 2 * LANES * b : 2 * LANES * b + REACH]
    decimated = split_dot(blocks[...], filt_ref)
    inside = lax.broadcasted_iota(jnp.int32, (channels, LANES), 1) < WLEN - (BLOCKS - 1) * LANES
    kept = []
    for w in range(WINDOWS):
        first = w * BLOCKS * channels
        last = first + (BLOCKS - 1) * channels
        kept += [decimated[first:last], jnp.where(inside, decimated[last : last + channels], 0.0)]
    decimated = jnp.concatenate(kept, axis=0)

    parts = split_dot(decimated, near_ref)
    sums_re, sums_im = [], []
    for w in range(WINDOWS):
        sum_re = sum_im = None
        for b in range(BLOCKS):
            row = (w * BLOCKS + b) * channels
            part_re = parts[row : row + channels, :NFREQ]
            part_im = parts[row : row + channels, NFREQ:]
            turn_re = far_ref[b : b + 1, :NFREQ]
            turn_im = far_ref[b : b + 1, NFREQ:]
            if b == 0:
                sum_re, sum_im = part_re, part_im
            else:
                sum_re = sum_re + (part_re * turn_re - part_im * turn_im)
                sum_im = sum_im + (part_re * turn_im + part_im * turn_re)
        sums_re.append(sum_re)
        sums_im.append(sum_im)
    spec_re = jnp.concatenate(sums_re, axis=0)
    spec_im = jnp.concatenate(sums_im, axis=0)
    own = whiten(spec_re, spec_im).astype(jnp.bfloat16).astype(jnp.float32)

    others = gathered.at[pl.ds(0, count - 1)]

    panel = min(count, 32)
    scale = 1.0 / math.sqrt(WINDOWS * NFREQ)

    loads[4].wait()
    pltpu.make_async_copy(others, others, recv_sem).wait()

    def work(index, carry):
        for j in range(panel):
            wide[j * SLOT : j * SLOT + WINDOWS * PIECES, :] = gathered[index * panel + j].astype(jnp.float32)
        half = PIECES // 2
        for i in range(half):
            real, imag = slice(LANES * i, LANES * (i + 1)), slice(NFREQ + LANES * i, NFREQ + LANES * (i + 1))
            b_re = [wide[pl.ds(w * PIECES + i, panel, stride=SLOT), :] for w in range(WINDOWS)]
            b_im = [wide[pl.ds(w * PIECES + half + i, panel, stride=SLOT), :] for w in range(WINDOWS)]
            for c in range(channels):
                cross_re = cross_im = None
                for w in range(WINDOWS):
                    a_re = own[w * channels + c : w * channels + c + 1, real]
                    a_im = own[w * channels + c : w * channels + c + 1, imag]
                    term_re = a_re * b_re[w] + a_im * b_im[w]
                    term_im = a_im * b_re[w] - a_re * b_im[w]
                    cross_re = term_re if w == 0 else cross_re + term_re
                    cross_im = term_im if w == 0 else cross_im + term_im
                cross[c * panel : (c + 1) * panel, real] = cross_re.astype(jnp.bfloat16)
                cross[c * panel : (c + 1) * panel, imag] = cross_im.astype(jnp.bfloat16)
        corr = jnp.dot(cross[...], inv_ref[...], preferred_element_type=jnp.float32) * scale
        corr = corr.astype(jnp.bfloat16)
        for c in range(channels):
            out_ref[c, pl.ds(pl.multiple_of(index * panel, panel), panel), :] = corr[c * panel : (c + 1) * panel]
        return carry

    if count == panel:
        work(0, 0)
    else:
        lax.fori_loop(0, count // panel, work, 0)
    pltpu.make_async_copy(others, others, send_sem).wait()


def solution(mesh):
    groups, members = mesh.shape["grp"], mesh.shape["mem"]
    count = groups * members
    tables = [
        filter_table(),
        halves(wave_table(np.arange(LANES))),
        np.tile(wave_table(LANES * np.arange(BLOCKS)), (WINDOWS, 1)).astype(np.float32),
        inverse_table(),
    ]

    def on_device(raw_traces):
        channels, length = raw_traces.shape
        start = 2 * WLEN * (WINDOWS - 1) // LANES * LANES
        operands = [
            pltpu.with_memory_space_constraint(x, pltpu.HBM)
            for x in [raw_traces] + [jnp.asarray(table) for table in tables]
        ]
        return pl.pallas_call(
            functools.partial(kernel, groups, members),
            out_shape=jax.ShapeDtypeStruct((channels, count, 2 * MAXLAG + 1), jnp.bfloat16),
            in_specs=[pl.BlockSpec(memory_space=pl.ANY)] * len(operands),
            out_specs=pl.BlockSpec(memory_space=pltpu.VMEM),
            scratch_shapes=[pltpu.VMEM(x.shape, x.dtype) for x in operands]
            + [
                pltpu.VMEM((channels, start + SPAN + LANES), jnp.float32),
                pltpu.VMEM((WINDOWS * BLOCKS, REACH), jnp.float32),
                pltpu.VMEM((WINDOWS * BLOCKS * channels, REACH), jnp.float32),
                pltpu.VMEM((count, WINDOWS * PIECES, LANES), jnp.bfloat16),
                pltpu.VMEM((min(count, 32) * SLOT, LANES), jnp.float32),
                pltpu.VMEM((min(count, 32) * channels, 2 * NFREQ), jnp.bfloat16),
                pltpu.SemaphoreType.DMA((len(operands),)),
                pltpu.SemaphoreType.DMA,
                pltpu.SemaphoreType.DMA,
            ],
            compiler_params=pltpu.CompilerParams(
                collective_id=0, has_side_effects=True, vmem_limit_bytes=VMEM_LIMIT
            ),
        )(*operands)

    return jax.shard_map(
        on_device,
        mesh=mesh,
        in_specs=(P(("grp", "mem"), None),),
        out_specs=P(("grp", "mem"), None, None),
        check_vma=False,
    )
```

```python
import functools
import math

import jax
import jax.numpy as jnp
import numpy as np
from jax import lax
from jax.experimental import pallas as pl
from jax.experimental.pallas import tpu as pltpu
from jax.sharding import PartitionSpec as P

WINDOWS = 2
WLEN = 1500
NFREQ = 384
TAPS = 32
MAXLAG = 200
LANES = 128
BLOCKS = -(-WLEN // LANES)
REACH = 3 * LANES
SPAN = 2 * LANES * (BLOCKS - 1) + REACH
PIECES = 2 * NFREQ // LANES
SLOT = 16
VMEM_LIMIT = 48 * 1024 * 1024
LOGICAL = pl.DeviceIdType.LOGICAL


def halves(table):
    high = table.astype(jnp.bfloat16)
    return np.stack([high, (table - high.astype(np.float64)).astype(jnp.bfloat16)])


def filter_table():
    k = np.arange(TAPS)
    window = 0.5 - 0.5 * np.cos(2.0 * np.pi * (k + 0.5) / TAPS)
    taps = 0.5 * np.sinc((k - (TAPS - 1) / 2.0) * 0.5) * window
    table = np.zeros((REACH, LANES))
    for n in range(LANES):
        table[2 * n : 2 * n + TAPS, n] = taps
    return halves(table)


def wave_table(times):
    phase = times[:, None] * np.arange(1, NFREQ + 1)[None, :] % WLEN
    angle = 2.0 * np.pi * phase / WLEN
    return np.concatenate([np.cos(angle), -np.sin(angle)], axis=1)


def inverse_table():
    shifts = np.arange(2 * MAXLAG + 1) - MAXLAG
    phase = np.mod(np.arange(1, NFREQ + 1)[:, None] * shifts[None, :], WLEN)
    angle = 2.0 * np.pi * phase / WLEN
    return np.concatenate([np.cos(angle), -np.sin(angle)], axis=0).astype(jnp.bfloat16)


def split_dot(left, right):
    high = left.astype(jnp.bfloat16)
    low = (left - high.astype(jnp.float32)).astype(jnp.bfloat16)
    return jnp.dot(jnp.concatenate([high, low, high], axis=1),
                   jnp.concatenate([right[0], right[0], right[1]], axis=0),
                   preferred_element_type=jnp.float32)


def whiten(spec_re, spec_im):
    power = spec_re * spec_re + spec_im * spec_im
    level = 0.01 * jnp.mean(power, axis=1, keepdims=True)
    factor = 1.0 / jnp.sqrt(power + level + 1e-06)
    return jnp.concatenate([spec_re * factor, spec_im * factor], axis=1)


def kernel(groups, members, *refs):
    operands, out_ref = refs[:5], refs[5]
    held, (padded, lead, blocks, gathered, wide, cross, load_sem, send_sem, recv_sem) = refs[6:11], refs[11:]
    raw_ref, filt_ref, near_ref, far_ref, inv_ref = held
    count = groups * members
    grp, mem = lax.axis_index("grp"), lax.axis_index("mem")
    me = grp * members + mem
    channels, length = raw_ref.shape

    loads = [pltpu.make_async_copy(operands[i], held[i], load_sem.at[i]) for i in range(5)]
    for load in loads:
        load.start()
    barrier = pltpu.get_barrier_semaphore()

    def peer_of(step):
        peer = me + step
        return jnp.where(peer >= count, peer - count, peer)

    def greet(step, carry):
        pl.semaphore_signal(barrier, inc=1, device_id=peer_of(step), device_id_type=LOGICAL)
        return carry

    lax.fori_loop(1, count, greet, 0)

    whole = length // LANES * LANES
    padded[:, whole:] = jnp.zeros((channels, padded.shape[1] - whole), jnp.float32)
    loads[0].wait()
    padded[:, :length] = raw_ref[...]
    pieces = []
    for w in range(WINDOWS):
        start = 2 * WLEN * w
        base = start // LANES * LANES
        if start == base:
            piece = padded[:, start : start + SPAN]
        else:
            width = SPAN + LANES
            piece = pltpu.roll(padded[:, base : base + width], width - (start - base), 1)
        pieces.append(piece)
        for b in range(BLOCKS):
            row = w * BLOCKS + b
            lead[row : row + 1, :] = piece[:1, 2 * LANES * b : 2 * LANES * b + REACH]

    loads[1].wait()
    first = split_dot(lead[...], filt_ref)
    row = lax.broadcasted_iota(jnp.int32, first.shape, 0)
    beyond = lax.broadcasted_iota(jnp.int32, first.shape, 1) >= WLEN - (BLOCKS - 1) * LANES
    first = jnp.where((lax.rem(row, BLOCKS) == BLOCKS - 1) & beyond, 0.0, first)
    loads[2].wait()
    parts = split_dot(first, near_ref)
    loads[3].wait()
    part_re, part_im = parts[:, :NFREQ], parts[:, NFREQ:]
    turn_re, turn_im = far_ref[:, :NFREQ], far_ref[:, NFREQ:]
    window = lax.broadcasted_iota(jnp.int32, part_re.shape, 0) // BLOCKS
    sums = []
    for turned in (part_re * turn_re - part_im * turn_im, part_re * turn_im + part_im * turn_re):
        sums.append(jnp.concatenate(
            [
                jnp.sum(jnp.where(window == w, turned, 0.0), axis=0, keepdims=True)
                for w in range(WINDOWS)
            ],
            axis=0,
        ))
    white = whiten(*sums)
    gathered[me] = jnp.concatenate(
        [
            white[w : w + 1, LANES * i : LANES * (i + 1)]
            for w in range(WINDOWS)
            for i in range(PIECES)
        ],
        axis=0,
    ).astype(jnp.bfloat16)

    pl.semaphore_wait(barrier, count - 1)

    def send(step, carry):
        pltpu.make_async_remote_copy(
            src_ref=gathered.at[me],
            dst_ref=gathered.at[me],
            send_sem=send_sem,
            recv_sem=recv_sem,
            device_id=peer_of(step),
            device_id_type=LOGICAL,
        ).start()
        return carry

    lax.fori_loop(1, count, send, 0)

    for w in range(WINDOWS):
        for b in range(BLOCKS):
            row = (w * BLOCKS + b) * channels
            blocks[row : row + channels, :] = pieces[w][:, 2 * LANES * b : 2 * LANES * b + REACH]
    decimated = split_dot(blocks[...], filt_ref)
    inside = lax.broadcasted_iota(jnp.int32, (channels, LANES), 1) < WLEN - (BLOCKS - 1) * LANES
    kept = []
    for w in range(WINDOWS):
        first = w * BLOCKS * channels
        last = first + (BLOCKS - 1) * channels
        kept += [decimated[first:last], jnp.where(inside, decimated[last : last + channels], 0.0)]
    decimated = jnp.concatenate(kept, axis=0)

    parts = split_dot(decimated, near_ref)
    sums_re, sums_im = [], []
    for w in range(WINDOWS):
        sum_re = sum_im = None
        for b in range(BLOCKS):
            row = (w * BLOCKS + b) * channels
            part_re = parts[row : row + channels, :NFREQ]
            part_im = parts[row : row + channels, NFREQ:]
            turn_re = far_ref[b : b + 1, :NFREQ]
            turn_im = far_ref[b : b + 1, NFREQ:]
            if b == 0:
                sum_re, sum_im = part_re, part_im
            else:
                sum_re = sum_re + (part_re * turn_re - part_im * turn_im)
                sum_im = sum_im + (part_re * turn_im + part_im * turn_re)
        sums_re.append(sum_re)
        sums_im.append(sum_im)
    spec_re = jnp.concatenate(sums_re, axis=0)
    spec_im = jnp.concatenate(sums_im, axis=0)
    own = whiten(spec_re, spec_im).astype(jnp.bfloat16).astype(jnp.float32)

    others = gathered.at[pl.ds(0, count - 1)]

    panel = min(count, 32)
    scale = 1.0 / math.sqrt(WINDOWS * NFREQ)

    loads[4].wait()
    pltpu.make_async_copy(others, others, recv_sem).wait()

    def work(index, carry):
        for j in range(panel):
            wide[j * SLOT : j * SLOT + WINDOWS * PIECES, :] = gathered[index * panel + j].astype(jnp.float32)
        half = PIECES // 2
        for i in range(half):
            real, imag = slice(LANES * i, LANES * (i + 1)), slice(NFREQ + LANES * i, NFREQ + LANES * (i + 1))
            b_re = [wide[pl.ds(w * PIECES + i, panel, stride=SLOT), :] for w in range(WINDOWS)]
            b_im = [wide[pl.ds(w * PIECES + half + i, panel, stride=SLOT), :] for w in range(WINDOWS)]
            for c in range(channels):
                cross_re = cross_im = None
                for w in range(WINDOWS):
                    a_re = own[w * channels + c : w * channels + c + 1, real]
                    a_im = own[w * channels + c : w * channels + c + 1, imag]
                    term_re = a_re * b_re[w] + a_im * b_im[w]
                    term_im = a_im * b_re[w] - a_re * b_im[w]
                    cross_re = term_re if w == 0 else cross_re + term_re
                    cross_im = term_im if w == 0 else cross_im + term_im
                cross[c * panel : (c + 1) * panel, real] = cross_re.astype(jnp.bfloat16)
                cross[c * panel : (c + 1) * panel, imag] = cross_im.astype(jnp.bfloat16)
        corr = jnp.dot(cross[...], inv_ref[...], preferred_element_type=jnp.float32) * scale
        corr = corr.astype(jnp.bfloat16)
        for c in range(channels):
            out_ref[c, pl.ds(pl.multiple_of(index * panel, panel), panel), :] = corr[c * panel : (c + 1) * panel]
        return carry

    if count == panel:
        work(0, 0)
    else:
        lax.fori_loop(0, count // panel, work, 0)
    pltpu.make_async_copy(others, others, send_sem).wait()


def solution(mesh):
    groups, members = mesh.shape["grp"], mesh.shape["mem"]
    count = groups * members
    tables = [
        filter_table(),
        halves(wave_table(np.arange(LANES))),
        np.tile(wave_table(LANES * np.arange(BLOCKS)), (WINDOWS, 1)).astype(np.float32),
        inverse_table(),
    ]

    def on_device(raw_traces):
        channels, length = raw_traces.shape
        start = 2 * WLEN * (WINDOWS - 1) // LANES * LANES
        operands = [
            pltpu.with_memory_space_constraint(x, pltpu.HBM)
            for x in [raw_traces] + [jnp.asarray(table) for table in tables]
        ]
        return pl.pallas_call(
            functools.partial(kernel, groups, members),
            out_shape=jax.ShapeDtypeStruct((channels, count, 2 * MAXLAG + 1), jnp.bfloat16),
            in_specs=[pl.BlockSpec(memory_space=pl.ANY)] * len(operands),
            out_specs=pl.BlockSpec(memory_space=pltpu.VMEM),
            scratch_shapes=[pltpu.VMEM(x.shape, x.dtype) for x in operands]
            + [
                pltpu.VMEM((channels, start + SPAN + LANES), jnp.float32),
                pltpu.VMEM((WINDOWS * BLOCKS, REACH), jnp.float32),
                pltpu.VMEM((WINDOWS * BLOCKS * channels, REACH), jnp.float32),
                pltpu.VMEM((count, WINDOWS * PIECES, LANES), jnp.bfloat16),
                pltpu.VMEM((min(count, 32) * SLOT, LANES), jnp.float32),
                pltpu.VMEM((min(count, 32) * channels, 2 * NFREQ), jnp.bfloat16),
                pltpu.SemaphoreType.DMA((len(operands),)),
                pltpu.SemaphoreType.DMA,
                pltpu.SemaphoreType.DMA,
            ],
            compiler_params=pltpu.CompilerParams(
                collective_id=0, has_side_effects=True, vmem_limit_bytes=VMEM_LIMIT
            ),
        )(*operands)

    return jax.shard_map(
        on_device,
        mesh=mesh,
        in_specs=(P(("grp", "mem"), None),),
        out_specs=P(("grp", "mem"), None, None),
        check_vma=False,
    )
```

```python
import functools
import math

import jax
import jax.numpy as jnp
import numpy as np
from jax import lax
from jax.experimental import pallas as pl
from jax.experimental.pallas import tpu as pltpu
from jax.sharding import PartitionSpec as P

WINDOWS = 2
WLEN = 1500
NFREQ = 384
TAPS = 32
MAXLAG = 200
LANES = 128
BLOCKS = -(-WLEN // LANES)
REACH = 3 * LANES
SPAN = 2 * LANES * (BLOCKS - 1) + REACH
PIECES = 2 * NFREQ // LANES
SLOT = 16
CHUNKS = 4
VMEM_LIMIT = 48 * 1024 * 1024
LOGICAL = pl.DeviceIdType.LOGICAL


def halves(table):
    high = table.astype(jnp.bfloat16)
    return np.stack([high, (table - high.astype(np.float64)).astype(jnp.bfloat16)])


def filter_table():
    k = np.arange(TAPS)
    window = 0.5 - 0.5 * np.cos(2.0 * np.pi * (k + 0.5) / TAPS)
    taps = 0.5 * np.sinc((k - (TAPS - 1) / 2.0) * 0.5) * window
    table = np.zeros((REACH, LANES))
    for n in range(LANES):
        table[2 * n : 2 * n + TAPS, n] = taps
    return halves(table)


def wave_table(times):
    phase = times[:, None] * np.arange(1, NFREQ + 1)[None, :] % WLEN
    angle = 2.0 * np.pi * phase / WLEN
    return np.concatenate([np.cos(angle), -np.sin(angle)], axis=1)


def inverse_table():
    shifts = np.arange(2 * MAXLAG + 1) - MAXLAG
    phase = np.mod(np.arange(1, NFREQ + 1)[:, None] * shifts[None, :], WLEN)
    angle = 2.0 * np.pi * phase / WLEN
    return np.concatenate([np.cos(angle), -np.sin(angle)], axis=0).astype(jnp.bfloat16)


def split_dot(left, right):
    high = left.astype(jnp.bfloat16)
    low = (left - high.astype(jnp.float32)).astype(jnp.bfloat16)
    return jnp.dot(jnp.concatenate([high, low, high], axis=1),
                   jnp.concatenate([right[0], right[0], right[1]], axis=0),
                   preferred_element_type=jnp.float32)


def whiten(spec_re, spec_im):
    power = spec_re * spec_re + spec_im * spec_im
    level = 0.01 * jnp.mean(power, axis=1, keepdims=True)
    factor = 1.0 / jnp.sqrt(power + level + 1e-06)
    return jnp.concatenate([spec_re * factor, spec_im * factor], axis=1)


def kernel(groups, members, *refs):
    operands, out_ref = refs[:5], refs[5]
    held, (padded, lead, blocks, gathered, wide, cross, load_sem, send_sem, recv_sem,
           pass_send_sem, pass_recv_sem) = refs[6:11], refs[11:]
    raw_ref, filt_ref, near_ref, far_ref, inv_ref = held
    count = groups * members
    grp, mem = lax.axis_index("grp"), lax.axis_index("mem")
    channels, length = raw_ref.shape

    loads = [pltpu.make_async_copy(operands[i], held[i], load_sem.at[i]) for i in range(5)]
    for load in loads:
        load.start()
    barrier = pltpu.get_barrier_semaphore()

    def wrap(position, size):
        return jnp.where(position >= size, position - size, position)

    def column_peer(step):
        return wrap(grp + step, groups) * members + mem

    def sibling(step):
        return grp * members + wrap(mem + step, members)

    def greet(step, carry):
        pl.semaphore_signal(barrier, inc=1, device_id=column_peer(step), device_id_type=LOGICAL)
        return carry

    lax.fori_loop(1, groups, greet, 0)
    for step in range(1, members):
        pl.semaphore_signal(barrier, inc=1, device_id=sibling(step), device_id_type=LOGICAL)

    whole = length // LANES * LANES
    padded[:, whole:] = jnp.zeros((channels, padded.shape[1] - whole), jnp.float32)
    loads[0].wait()
    padded[:, :length] = raw_ref[...]
    pieces = []
    for w in range(WINDOWS):
        start = 2 * WLEN * w
        base = start // LANES * LANES
        if start == base:
            piece = padded[:, start : start + SPAN]
        else:
            width = SPAN + LANES
            piece = pltpu.roll(padded[:, base : base + width], width - (start - base), 1)
        pieces.append(piece)
        for b in range(BLOCKS):
            row = w * BLOCKS + b
            lead[row : row + 1, :] = piece[:1, 2 * LANES * b : 2 * LANES * b + REACH]

    loads[1].wait()
    first = split_dot(lead[...], filt_ref)
    row = lax.broadcasted_iota(jnp.int32, first.shape, 0)
    beyond = lax.broadcasted_iota(jnp.int32, first.shape, 1) >= WLEN - (BLOCKS - 1) * LANES
    first = jnp.where((lax.rem(row, BLOCKS) == BLOCKS - 1) & beyond, 0.0, first)
    loads[2].wait()
    parts = split_dot(first, near_ref)
    loads[3].wait()
    part_re, part_im = parts[:, :NFREQ], parts[:, NFREQ:]
    turn_re, turn_im = far_ref[:, :NFREQ], far_ref[:, NFREQ:]
    window = lax.broadcasted_iota(jnp.int32, part_re.shape, 0) // BLOCKS
    sums = []
    for turned in (part_re * turn_re - part_im * turn_im, part_re * turn_im + part_im * turn_re):
        sums.append(jnp.concatenate(
            [
                jnp.sum(jnp.where(window == w, turned, 0.0), axis=0, keepdims=True)
                for w in range(WINDOWS)
            ],
            axis=0,
        ))
    white = whiten(*sums)
    gathered[mem, grp] = jnp.concatenate(
        [
            white[w : w + 1, LANES * i : LANES * (i + 1)]
            for w in range(WINDOWS)
            for i in range(PIECES)
        ],
        axis=0,
    ).astype(jnp.bfloat16)

    pl.semaphore_wait(barrier, groups + members - 2)
    chunk = groups // CHUNKS
    mine = grp // chunk

    def send(step, carry):
        pltpu.make_async_remote_copy(
            src_ref=gathered.at[mem, grp],
            dst_ref=gathered.at[mem, grp],
            send_sem=send_sem,
            recv_sem=recv_sem.at[mine],
            device_id=column_peer(step),
            device_id_type=LOGICAL,
        ).start()
        return carry

    lax.fori_loop(1, groups, send, 0)

    for w in range(WINDOWS):
        for b in range(BLOCKS):
            row = (w * BLOCKS + b) * channels
            blocks[row : row + channels, :] = pieces[w][:, 2 * LANES * b : 2 * LANES * b + REACH]
    decimated = split_dot(blocks[...], filt_ref)
    inside = lax.broadcasted_iota(jnp.int32, (channels, LANES), 1) < WLEN - (BLOCKS - 1) * LANES
    kept = []
    for w in range(WINDOWS):
        first = w * BLOCKS * channels
        last = first + (BLOCKS - 1) * channels
        kept += [decimated[first:last], jnp.where(inside, decimated[last : last + channels], 0.0)]
    decimated = jnp.concatenate(kept, axis=0)

    parts = split_dot(decimated, near_ref)
    sums_re, sums_im = [], []
    for w in range(WINDOWS):
        sum_re = sum_im = None
        for b in range(BLOCKS):
            row = (w * BLOCKS + b) * channels
            part_re = parts[row : row + channels, :NFREQ]
            part_im = parts[row : row + channels, NFREQ:]
            turn_re = far_ref[b : b + 1, :NFREQ]
            turn_im = far_ref[b : b + 1, NFREQ:]
            if b == 0:
                sum_re, sum_im = part_re, part_im
            else:
                sum_re = sum_re + (part_re * turn_re - part_im * turn_im)
                sum_im = sum_im + (part_re * turn_im + part_im * turn_re)
        sums_re.append(sum_re)
        sums_im.append(sum_im)
    spec_re = jnp.concatenate(sums_re, axis=0)
    spec_im = jnp.concatenate(sums_im, axis=0)
    own = whiten(spec_re, spec_im).astype(jnp.bfloat16).astype(jnp.float32)

    def await_bytes(ref, sem):
        pltpu.make_async_copy(ref, ref, sem).wait()

    await_bytes(gathered.at[0, pl.ds(0, chunk - 1)], recv_sem.at[mine])
    for i in range(CHUNKS):
        part = wrap(mine + i, CHUNKS)
        if i > 0:
            await_bytes(gathered.at[0, pl.ds(0, chunk)], recv_sem.at[part])
        held_part = gathered.at[mem, pl.ds(part * chunk, chunk)]
        for step in range(1, members):
            pltpu.make_async_remote_copy(
                src_ref=held_part,
                dst_ref=held_part,
                send_sem=pass_send_sem,
                recv_sem=pass_recv_sem,
                device_id=sibling(step),
                device_id_type=LOGICAL,
            ).start()

    panel = min(count, 32)
    scale = 1.0 / math.sqrt(WINDOWS * NFREQ)

    loads[4].wait()
    await_bytes(gathered.at[pl.ds(0, members - 1)], pass_recv_sem)

    def work(index, carry):
        for j in range(panel):
            wide[j * SLOT : j * SLOT + WINDOWS * PIECES, :] = gathered[
                j % members, index * (panel // members) + j // members
            ].astype(jnp.float32)
        half = PIECES // 2
        for i in range(half):
            real, imag = slice(LANES * i, LANES * (i + 1)), slice(NFREQ + LANES * i, NFREQ + LANES * (i + 1))
            b_re = [wide[pl.ds(w * PIECES + i, panel, stride=SLOT), :] for w in range(WINDOWS)]
            b_im = [wide[pl.ds(w * PIECES + half + i, panel, stride=SLOT), :] for w in range(WINDOWS)]
            for c in range(channels):
                cross_re = cross_im = None
                for w in range(WINDOWS):
                    a_re = own[w * channels + c : w * channels + c + 1, real]
                    a_im = own[w * channels + c : w * channels + c + 1, imag]
                    term_re = a_re * b_re[w] + a_im * b_im[w]
                    term_im = a_im * b_re[w] - a_re * b_im[w]
                    cross_re = term_re if w == 0 else cross_re + term_re
                    cross_im = term_im if w == 0 else cross_im + term_im
                cross[c * panel : (c + 1) * panel, real] = cross_re.astype(jnp.bfloat16)
                cross[c * panel : (c + 1) * panel, imag] = cross_im.astype(jnp.bfloat16)
        corr = jnp.dot(cross[...], inv_ref[...], preferred_element_type=jnp.float32) * scale
        corr = corr.astype(jnp.bfloat16)
        for c in range(channels):
            out_ref[c, pl.ds(pl.multiple_of(index * panel, panel), panel), :] = corr[c * panel : (c + 1) * panel]
        return carry

    if count == panel:
        work(0, 0)
    else:
        lax.fori_loop(0, count // panel, work, 0)
    await_bytes(gathered.at[0, pl.ds(0, groups - 1)], send_sem)
    await_bytes(gathered.at[pl.ds(0, members - 1)], pass_send_sem)


def solution(mesh):
    groups, members = mesh.shape["grp"], mesh.shape["mem"]
    count = groups * members
    tables = [
        filter_table(),
        halves(wave_table(np.arange(LANES))),
        np.tile(wave_table(LANES * np.arange(BLOCKS)), (WINDOWS, 1)).astype(np.float32),
        inverse_table(),
    ]

    def on_device(raw_traces):
        channels, length = raw_traces.shape
        start = 2 * WLEN * (WINDOWS - 1) // LANES * LANES
        operands = [
            pltpu.with_memory_space_constraint(x, pltpu.HBM)
            for x in [raw_traces] + [jnp.asarray(table) for table in tables]
        ]
        return pl.pallas_call(
            functools.partial(kernel, groups, members),
            out_shape=jax.ShapeDtypeStruct((channels, count, 2 * MAXLAG + 1), jnp.bfloat16),
            in_specs=[pl.BlockSpec(memory_space=pl.ANY)] * len(operands),
            out_specs=pl.BlockSpec(memory_space=pltpu.VMEM),
            scratch_shapes=[pltpu.VMEM(x.shape, x.dtype) for x in operands]
            + [
                pltpu.VMEM((channels, start + SPAN + LANES), jnp.float32),
                pltpu.VMEM((WINDOWS * BLOCKS, REACH), jnp.float32),
                pltpu.VMEM((WINDOWS * BLOCKS * channels, REACH), jnp.float32),
                pltpu.VMEM((members, groups, WINDOWS * PIECES, LANES), jnp.bfloat16),
                pltpu.VMEM((min(count, 32) * SLOT, LANES), jnp.float32),
                pltpu.VMEM((min(count, 32) * channels, 2 * NFREQ), jnp.bfloat16),
                pltpu.SemaphoreType.DMA((len(operands),)),
                pltpu.SemaphoreType.DMA,
                pltpu.SemaphoreType.DMA((CHUNKS,)),
                pltpu.SemaphoreType.DMA,
                pltpu.SemaphoreType.DMA,
            ],
            compiler_params=pltpu.CompilerParams(
                collective_id=0, has_side_effects=True, vmem_limit_bytes=VMEM_LIMIT
            ),
        )(*operands)

    return jax.shard_map(
        on_device,
        mesh=mesh,
        in_specs=(P(("grp", "mem"), None),),
        out_specs=P(("grp", "mem"), None, None),
        check_vma=False,
    )
```

```python
import functools
import math

import jax
import jax.numpy as jnp
import numpy as np
from jax import lax
from jax.experimental import pallas as pl
from jax.experimental.pallas import tpu as pltpu
from jax.sharding import PartitionSpec as P

WINDOWS = 2
WLEN = 1500
NFREQ = 384
TAPS = 32
MAXLAG = 200
LANES = 128
BLOCKS = -(-WLEN // LANES)
REACH = 3 * LANES
SPAN = 2 * LANES * (BLOCKS - 1) + REACH
PIECES = 2 * NFREQ // LANES
SLOT = 16
HALVES = 2
VMEM_LIMIT = 48 * 1024 * 1024
LOGICAL = pl.DeviceIdType.LOGICAL


def halves(table):
    high = table.astype(jnp.bfloat16)
    return np.stack([high, (table - high.astype(np.float64)).astype(jnp.bfloat16)])


def filter_table():
    k = np.arange(TAPS)
    window = 0.5 - 0.5 * np.cos(2.0 * np.pi * (k + 0.5) / TAPS)
    taps = 0.5 * np.sinc((k - (TAPS - 1) / 2.0) * 0.5) * window
    table = np.zeros((REACH, LANES))
    for n in range(LANES):
        table[2 * n : 2 * n + TAPS, n] = taps
    return halves(table)


def wave_table(times):
    phase = times[:, None] * np.arange(1, NFREQ + 1)[None, :] % WLEN
    angle = 2.0 * np.pi * phase / WLEN
    return np.concatenate([np.cos(angle), -np.sin(angle)], axis=1)


def inverse_table():
    shifts = np.arange(2 * MAXLAG + 1) - MAXLAG
    phase = np.mod(np.arange(1, NFREQ + 1)[:, None] * shifts[None, :], WLEN)
    angle = 2.0 * np.pi * phase / WLEN
    return np.concatenate([np.cos(angle), -np.sin(angle)], axis=0).astype(jnp.bfloat16)


def split_dot(left, right):
    high = left.astype(jnp.bfloat16)
    low = (left - high.astype(jnp.float32)).astype(jnp.bfloat16)
    return jnp.dot(jnp.concatenate([high, low, high], axis=1),
                   jnp.concatenate([right[0], right[0], right[1]], axis=0),
                   preferred_element_type=jnp.float32)


def whiten(spec_re, spec_im):
    power = spec_re * spec_re + spec_im * spec_im
    level = 0.01 * jnp.mean(power, axis=1, keepdims=True)
    factor = 1.0 / jnp.sqrt(power + level + 1e-06)
    return jnp.concatenate([spec_re * factor, spec_im * factor], axis=1)


def kernel(groups, members, *refs):
    operands, out_ref = refs[:5], refs[5]
    held, (padded, lead, blocks, gathered, wide, cross, load_sem, send_sem, recv_sem) = refs[6:11], refs[11:]
    raw_ref, filt_ref, near_ref, far_ref, inv_ref = held
    count = groups * members
    grp, mem = lax.axis_index("grp"), lax.axis_index("mem")
    me = grp * members + mem
    channels, length = raw_ref.shape

    loads = [pltpu.make_async_copy(operands[i], held[i], load_sem.at[i]) for i in range(5)]
    for load in loads[:4]:
        load.start()
    barrier = pltpu.get_barrier_semaphore()

    def peer_of(step):
        peer = me + step
        return jnp.where(peer >= count, peer - count, peer)

    def greet(step, carry):
        pl.semaphore_signal(barrier, inc=1, device_id=peer_of(step), device_id_type=LOGICAL)
        return carry

    lax.fori_loop(1, count, greet, 0)

    whole = length // LANES * LANES
    padded[:, whole:] = jnp.zeros((channels, padded.shape[1] - whole), jnp.float32)
    loads[0].wait()
    padded[:, :length] = raw_ref[...]
    pieces = []
    for w in range(WINDOWS):
        start = 2 * WLEN * w
        base = start // LANES * LANES
        if start == base:
            piece = padded[:, start : start + SPAN]
        else:
            width = SPAN + LANES
            piece = pltpu.roll(padded[:, base : base + width], width - (start - base), 1)
        pieces.append(piece)
        for b in range(BLOCKS):
            row = w * BLOCKS + b
            lead[row : row + 1, :] = piece[:1, 2 * LANES * b : 2 * LANES * b + REACH]

    loads[1].wait()
    first = split_dot(lead[...], filt_ref)
    row = lax.broadcasted_iota(jnp.int32, first.shape, 0)
    beyond = lax.broadcasted_iota(jnp.int32, first.shape, 1) >= WLEN - (BLOCKS - 1) * LANES
    first = jnp.where((lax.rem(row, BLOCKS) == BLOCKS - 1) & beyond, 0.0, first)
    loads[2].wait()
    parts = split_dot(first, near_ref)
    loads[3].wait()
    part_re, part_im = parts[:, :NFREQ], parts[:, NFREQ:]
    turn_re, turn_im = far_ref[:, :NFREQ], far_ref[:, NFREQ:]
    window = lax.broadcasted_iota(jnp.int32, part_re.shape, 0) // BLOCKS
    sums = []
    for turned in (part_re * turn_re - part_im * turn_im, part_re * turn_im + part_im * turn_re):
        sums.append(jnp.concatenate(
            [
                jnp.sum(jnp.where(window == w, turned, 0.0), axis=0, keepdims=True)
                for w in range(WINDOWS)
            ],
            axis=0,
        ))
    white = whiten(*sums)
    gathered[me] = jnp.concatenate(
        [
            white[w : w + 1, LANES * i : LANES * (i + 1)]
            for w in range(WINDOWS)
            for i in range(PIECES)
        ],
        axis=0,
    ).astype(jnp.bfloat16)

    pl.semaphore_wait(barrier, count - 1)

    half = count // HALVES
    mine = me // half

    def send(step, carry):
        pltpu.make_async_remote_copy(
            src_ref=gathered.at[me],
            dst_ref=gathered.at[me],
            send_sem=send_sem,
            recv_sem=recv_sem.at[mine],
            device_id=peer_of(step),
            device_id_type=LOGICAL,
        ).start()
        return carry

    lax.fori_loop(1, count, send, 0)

    loads[4].start()

    for w in range(WINDOWS):
        for b in range(BLOCKS):
            row = (w * BLOCKS + b) * channels
            blocks[row : row + channels, :] = pieces[w][:, 2 * LANES * b : 2 * LANES * b + REACH]
    decimated = split_dot(blocks[...], filt_ref)
    inside = lax.broadcasted_iota(jnp.int32, (channels, LANES), 1) < WLEN - (BLOCKS - 1) * LANES
    kept = []
    for w in range(WINDOWS):
        first = w * BLOCKS * channels
        last = first + (BLOCKS - 1) * channels
        kept += [decimated[first:last], jnp.where(inside, decimated[last : last + channels], 0.0)]
    decimated = jnp.concatenate(kept, axis=0)

    parts = split_dot(decimated, near_ref)
    sums_re, sums_im = [], []
    for w in range(WINDOWS):
        sum_re = sum_im = None
        for b in range(BLOCKS):
            row = (w * BLOCKS + b) * channels
            part_re = parts[row : row + channels, :NFREQ]
            part_im = parts[row : row + channels, NFREQ:]
            turn_re = far_ref[b : b + 1, :NFREQ]
            turn_im = far_ref[b : b + 1, NFREQ:]
            if b == 0:
                sum_re, sum_im = part_re, part_im
            else:
                sum_re = sum_re + (part_re * turn_re - part_im * turn_im)
                sum_im = sum_im + (part_re * turn_im + part_im * turn_re)
        sums_re.append(sum_re)
        sums_im.append(sum_im)
    spec_re = jnp.concatenate(sums_re, axis=0)
    spec_im = jnp.concatenate(sums_im, axis=0)
    own = whiten(spec_re, spec_im).astype(jnp.bfloat16).astype(jnp.float32)

    panel = min(half, 32)
    scale = 1.0 / math.sqrt(WINDOWS * NFREQ)

    def work(index, carry):
        for j in range(panel):
            wide[j * SLOT : j * SLOT + WINDOWS * PIECES, :] = gathered[index * panel + j].astype(jnp.float32)
        half = PIECES // 2
        for i in range(half):
            real, imag = slice(LANES * i, LANES * (i + 1)), slice(NFREQ + LANES * i, NFREQ + LANES * (i + 1))
            b_re = [wide[pl.ds(w * PIECES + i, panel, stride=SLOT), :] for w in range(WINDOWS)]
            b_im = [wide[pl.ds(w * PIECES + half + i, panel, stride=SLOT), :] for w in range(WINDOWS)]
            for c in range(channels):
                cross_re = cross_im = None
                for w in range(WINDOWS):
                    a_re = own[w * channels + c : w * channels + c + 1, real]
                    a_im = own[w * channels + c : w * channels + c + 1, imag]
                    term_re = a_re * b_re[w] + a_im * b_im[w]
                    term_im = a_im * b_re[w] - a_re * b_im[w]
                    cross_re = term_re if w == 0 else cross_re + term_re
                    cross_im = term_im if w == 0 else cross_im + term_im
                cross[c * panel : (c + 1) * panel, real] = cross_re.astype(jnp.bfloat16)
                cross[c * panel : (c + 1) * panel, imag] = cross_im.astype(jnp.bfloat16)
        corr = jnp.dot(cross[...], inv_ref[...], preferred_element_type=jnp.float32) * scale
        corr = corr.astype(jnp.bfloat16)
        for c in range(channels):
            out_ref[c, pl.ds(pl.multiple_of(index * panel, panel), panel), :] = corr[c * panel : (c + 1) * panel]
        return carry

    loads[4].wait()
    for i in range(HALVES):
        part = mine + i
        part = jnp.where(part >= HALVES, part - HALVES, part)
        arrived = gathered.at[pl.ds(0, half - 1 if i == 0 else half)]
        pltpu.make_async_copy(arrived, arrived, recv_sem.at[part]).wait()
        if half == panel:
            work(part, 0)
        else:
            panels = half // panel
            lax.fori_loop(part * panels, (part + 1) * panels, work, 0)
    others = gathered.at[pl.ds(0, count - 1)]
    pltpu.make_async_copy(others, others, send_sem).wait()


def solution(mesh):
    groups, members = mesh.shape["grp"], mesh.shape["mem"]
    count = groups * members
    tables = [
        filter_table(),
        halves(wave_table(np.arange(LANES))),
        np.tile(wave_table(LANES * np.arange(BLOCKS)), (WINDOWS, 1)).astype(np.float32),
        inverse_table(),
    ]

    def on_device(raw_traces):
        channels, length = raw_traces.shape
        start = 2 * WLEN * (WINDOWS - 1) // LANES * LANES
        operands = [
            pltpu.with_memory_space_constraint(x, pltpu.HBM)
            for x in [raw_traces] + [jnp.asarray(table) for table in tables]
        ]
        return pl.pallas_call(
            functools.partial(kernel, groups, members),
            out_shape=jax.ShapeDtypeStruct((channels, count, 2 * MAXLAG + 1), jnp.bfloat16),
            in_specs=[pl.BlockSpec(memory_space=pl.ANY)] * len(operands),
            out_specs=pl.BlockSpec(memory_space=pltpu.VMEM),
            scratch_shapes=[pltpu.VMEM(x.shape, x.dtype) for x in operands]
            + [
                pltpu.VMEM((channels, start + SPAN + LANES), jnp.float32),
                pltpu.VMEM((WINDOWS * BLOCKS, REACH), jnp.float32),
                pltpu.VMEM((WINDOWS * BLOCKS * channels, REACH), jnp.float32),
                pltpu.VMEM((count, WINDOWS * PIECES, LANES), jnp.bfloat16),
                pltpu.VMEM((min(count // HALVES, 32) * SLOT, LANES), jnp.float32),
                pltpu.VMEM((min(count // HALVES, 32) * channels, 2 * NFREQ), jnp.bfloat16),
                pltpu.SemaphoreType.DMA((len(operands),)),
                pltpu.SemaphoreType.DMA,
                pltpu.SemaphoreType.DMA((HALVES,)),
            ],
            compiler_params=pltpu.CompilerParams(
                collective_id=0, has_side_effects=True, vmem_limit_bytes=VMEM_LIMIT
            ),
        )(*operands)

    return jax.shard_map(
        on_device,
        mesh=mesh,
        in_specs=(P(("grp", "mem"), None),),
        out_specs=P(("grp", "mem"), None, None),
        check_vma=False,
    )
```

```python
import functools
import math

import jax
import jax.numpy as jnp
import numpy as np
from jax import lax
from jax.experimental import pallas as pl
from jax.experimental.pallas import tpu as pltpu
from jax.sharding import PartitionSpec as P

WINDOWS = 2
WLEN = 1500
NFREQ = 384
TAPS = 32
MAXLAG = 200
LANES = 128
BLOCKS = -(-WLEN // LANES)
REACH = 3 * LANES
SPAN = 2 * LANES * (BLOCKS - 1) + REACH
PIECES = 2 * NFREQ // LANES
SLOT = 16
HALVES = 2
VMEM_LIMIT = 48 * 1024 * 1024
LOGICAL = pl.DeviceIdType.LOGICAL


def halves(table):
    high = table.astype(jnp.bfloat16)
    return np.stack([high, (table - high.astype(np.float64)).astype(jnp.bfloat16)])


def filter_table():
    k = np.arange(TAPS)
    window = 0.5 - 0.5 * np.cos(2.0 * np.pi * (k + 0.5) / TAPS)
    taps = 0.5 * np.sinc((k - (TAPS - 1) / 2.0) * 0.5) * window
    table = np.zeros((REACH, LANES))
    for n in range(LANES):
        table[2 * n : 2 * n + TAPS, n] = taps
    return halves(table)


def wave_table(times):
    phase = times[:, None] * np.arange(1, NFREQ + 1)[None, :] % WLEN
    angle = 2.0 * np.pi * phase / WLEN
    return np.concatenate([np.cos(angle), -np.sin(angle)], axis=1)


def inverse_table():
    shifts = np.arange(2 * MAXLAG + 1) - MAXLAG
    phase = np.mod(np.arange(1, NFREQ + 1)[:, None] * shifts[None, :], WLEN)
    angle = 2.0 * np.pi * phase / WLEN
    return np.concatenate([np.cos(angle), -np.sin(angle)], axis=0).astype(jnp.bfloat16)


def split_dot(left, right):
    high = left.astype(jnp.bfloat16)
    low = (left - high.astype(jnp.float32)).astype(jnp.bfloat16)
    return jnp.dot(jnp.concatenate([high, low, high], axis=1),
                   jnp.concatenate([right[0], right[0], right[1]], axis=0),
                   preferred_element_type=jnp.float32)


def whiten(spec_re, spec_im):
    power = spec_re * spec_re + spec_im * spec_im
    level = 0.01 * jnp.mean(power, axis=1, keepdims=True)
    factor = 1.0 / jnp.sqrt(power + level + 1e-06)
    return jnp.concatenate([spec_re * factor, spec_im * factor], axis=1)


def kernel(groups, members, *refs):
    operands, out_ref = refs[:5], refs[5]
    held, (padded, lead, blocks, gathered, wide, cross, load_sem, send_sem, recv_sem) = refs[6:11], refs[11:]
    raw_ref, filt_ref, near_ref, far_ref, inv_ref = held
    count = groups * members
    grp, mem = lax.axis_index("grp"), lax.axis_index("mem")
    me = grp * members + mem
    channels, length = raw_ref.shape

    loads = [pltpu.make_async_copy(operands[i], held[i], load_sem.at[i]) for i in range(5)]
    for load in loads[:4]:
        load.start()
    barrier = pltpu.get_barrier_semaphore()

    def peer_of(step):
        peer = me + step
        return jnp.where(peer >= count, peer - count, peer)

    def greet(step, carry):
        pl.semaphore_signal(barrier, inc=1, device_id=peer_of(step), device_id_type=LOGICAL)
        return carry

    lax.fori_loop(1, count, greet, 0, unroll=count <= 32)

    whole = length // LANES * LANES
    padded[:, whole:] = jnp.zeros((channels, padded.shape[1] - whole), jnp.float32)
    loads[0].wait()
    padded[:, :length] = raw_ref[...]
    pieces = []
    for w in range(WINDOWS):
        start = 2 * WLEN * w
        base = start // LANES * LANES
        if start == base:
            piece = padded[:, start : start + SPAN]
        else:
            width = SPAN + LANES
            piece = pltpu.roll(padded[:, base : base + width], width - (start - base), 1)
        pieces.append(piece)
        for b in range(BLOCKS):
            row = w * BLOCKS + b
            lead[row : row + 1, :] = piece[:1, 2 * LANES * b : 2 * LANES * b + REACH]

    loads[1].wait()
    first = split_dot(lead[...], filt_ref)
    row = lax.broadcasted_iota(jnp.int32, first.shape, 0)
    beyond = lax.broadcasted_iota(jnp.int32, first.shape, 1) >= WLEN - (BLOCKS - 1) * LANES
    first = jnp.where((lax.rem(row, BLOCKS) == BLOCKS - 1) & beyond, 0.0, first)
    loads[2].wait()
    parts = split_dot(first, near_ref)
    loads[3].wait()
    part_re, part_im = parts[:, :NFREQ], parts[:, NFREQ:]
    turn_re, turn_im = far_ref[:, :NFREQ], far_ref[:, NFREQ:]
    window = lax.broadcasted_iota(jnp.int32, part_re.shape, 0) // BLOCKS
    sums = []
    for turned in (part_re * turn_re - part_im * turn_im, part_re * turn_im + part_im * turn_re):
        sums.append(jnp.concatenate(
            [
                jnp.sum(jnp.where(window == w, turned, 0.0), axis=0, keepdims=True)
                for w in range(WINDOWS)
            ],
            axis=0,
        ))
    white = whiten(*sums)
    gathered[me] = jnp.concatenate(
        [
            white[w : w + 1, LANES * i : LANES * (i + 1)]
            for w in range(WINDOWS)
            for i in range(PIECES)
        ],
        axis=0,
    ).astype(jnp.bfloat16)

    pl.semaphore_wait(barrier, count - 1)

    half = count // HALVES
    mine = me // half

    def send(step, carry):
        pltpu.make_async_remote_copy(
            src_ref=gathered.at[me],
            dst_ref=gathered.at[me],
            send_sem=send_sem,
            recv_sem=recv_sem.at[mine],
            device_id=peer_of(step),
            device_id_type=LOGICAL,
        ).start()
        return carry

    lax.fori_loop(1, count, send, 0, unroll=count <= 32)

    loads[4].start()

    for w in range(WINDOWS):
        for b in range(BLOCKS):
            row = (w * BLOCKS + b) * channels
            blocks[row : row + channels, :] = pieces[w][:, 2 * LANES * b : 2 * LANES * b + REACH]
    decimated = split_dot(blocks[...], filt_ref)
    inside = lax.broadcasted_iota(jnp.int32, (channels, LANES), 1) < WLEN - (BLOCKS - 1) * LANES
    kept = []
    for w in range(WINDOWS):
        first = w * BLOCKS * channels
        last = first + (BLOCKS - 1) * channels
        kept += [decimated[first:last], jnp.where(inside, decimated[last : last + channels], 0.0)]
    decimated = jnp.concatenate(kept, axis=0)

    parts = split_dot(decimated, near_ref)
    sums_re, sums_im = [], []
    for w in range(WINDOWS):
        sum_re = sum_im = None
        for b in range(BLOCKS):
            row = (w * BLOCKS + b) * channels
            part_re = parts[row : row + channels, :NFREQ]
            part_im = parts[row : row + channels, NFREQ:]
            turn_re = far_ref[b : b + 1, :NFREQ]
            turn_im = far_ref[b : b + 1, NFREQ:]
            if b == 0:
                sum_re, sum_im = part_re, part_im
            else:
                sum_re = sum_re + (part_re * turn_re - part_im * turn_im)
                sum_im = sum_im + (part_re * turn_im + part_im * turn_re)
        sums_re.append(sum_re)
        sums_im.append(sum_im)
    spec_re = jnp.concatenate(sums_re, axis=0)
    spec_im = jnp.concatenate(sums_im, axis=0)
    own = whiten(spec_re, spec_im).astype(jnp.bfloat16).astype(jnp.float32)

    panel = min(half, 32)
    scale = 1.0 / math.sqrt(WINDOWS * NFREQ)

    def work(index, carry):
        for j in range(panel):
            wide[j * SLOT : j * SLOT + WINDOWS * PIECES, :] = gathered[index * panel + j].astype(jnp.float32)
        half = PIECES // 2
        for i in range(half):
            real, imag = slice(LANES * i, LANES * (i + 1)), slice(NFREQ + LANES * i, NFREQ + LANES * (i + 1))
            b_re = [wide[pl.ds(w * PIECES + i, panel, stride=SLOT), :] for w in range(WINDOWS)]
            b_im = [wide[pl.ds(w * PIECES + half + i, panel, stride=SLOT), :] for w in range(WINDOWS)]
            for c in range(channels):
                cross_re = cross_im = None
                for w in range(WINDOWS):
                    a_re = own[w * channels + c : w * channels + c + 1, real]
                    a_im = own[w * channels + c : w * channels + c + 1, imag]
                    term_re = a_re * b_re[w] + a_im * b_im[w]
                    term_im = a_im * b_re[w] - a_re * b_im[w]
                    cross_re = term_re if w == 0 else cross_re + term_re
                    cross_im = term_im if w == 0 else cross_im + term_im
                cross[c * panel : (c + 1) * panel, real] = cross_re.astype(jnp.bfloat16)
                cross[c * panel : (c + 1) * panel, imag] = cross_im.astype(jnp.bfloat16)
        corr = jnp.dot(cross[...], inv_ref[...], preferred_element_type=jnp.float32) * scale
        corr = corr.astype(jnp.bfloat16)
        for c in range(channels):
            out_ref[c, pl.ds(pl.multiple_of(index * panel, panel), panel), :] = corr[c * panel : (c + 1) * panel]
        return carry

    loads[4].wait()
    for i in range(HALVES):
        part = mine + i
        part = jnp.where(part >= HALVES, part - HALVES, part)
        arrived = gathered.at[pl.ds(0, half - 1 if i == 0 else half)]
        pltpu.make_async_copy(arrived, arrived, recv_sem.at[part]).wait()
        if half == panel:
            work(part, 0)
        else:
            panels = half // panel
            lax.fori_loop(part * panels, (part + 1) * panels, work, 0)
    others = gathered.at[pl.ds(0, count - 1)]
    pltpu.make_async_copy(others, others, send_sem).wait()


def solution(mesh):
    groups, members = mesh.shape["grp"], mesh.shape["mem"]
    count = groups * members
    tables = [
        filter_table(),
        halves(wave_table(np.arange(LANES))),
        np.tile(wave_table(LANES * np.arange(BLOCKS)), (WINDOWS, 1)).astype(np.float32),
        inverse_table(),
    ]

    def on_device(raw_traces):
        channels, length = raw_traces.shape
        start = 2 * WLEN * (WINDOWS - 1) // LANES * LANES
        operands = [
            pltpu.with_memory_space_constraint(x, pltpu.HBM)
            for x in [raw_traces] + [jnp.asarray(table) for table in tables]
        ]
        return pl.pallas_call(
            functools.partial(kernel, groups, members),
            out_shape=jax.ShapeDtypeStruct((channels, count, 2 * MAXLAG + 1), jnp.bfloat16),
            in_specs=[pl.BlockSpec(memory_space=pl.ANY)] * len(operands),
            out_specs=pl.BlockSpec(memory_space=pltpu.VMEM),
            scratch_shapes=[pltpu.VMEM(x.shape, x.dtype) for x in operands]
            + [
                pltpu.VMEM((channels, start + SPAN + LANES), jnp.float32),
                pltpu.VMEM((WINDOWS * BLOCKS, REACH), jnp.float32),
                pltpu.VMEM((WINDOWS * BLOCKS * channels, REACH), jnp.float32),
                pltpu.VMEM((count, WINDOWS * PIECES, LANES), jnp.bfloat16),
                pltpu.VMEM((min(count // HALVES, 32) * SLOT, LANES), jnp.float32),
                pltpu.VMEM((min(count // HALVES, 32) * channels, 2 * NFREQ), jnp.bfloat16),
                pltpu.SemaphoreType.DMA((len(operands),)),
                pltpu.SemaphoreType.DMA,
                pltpu.SemaphoreType.DMA((HALVES,)),
            ],
            compiler_params=pltpu.CompilerParams(
                collective_id=0, has_side_effects=True, vmem_limit_bytes=VMEM_LIMIT
            ),
        )(*operands)

    return jax.shard_map(
        on_device,
        mesh=mesh,
        in_specs=(P(("grp", "mem"), None),),
        out_specs=P(("grp", "mem"), None, None),
        check_vma=False,
    )
```

```python
import functools
import math

import jax
import jax.numpy as jnp
import numpy as np
from jax import lax
from jax.experimental import pallas as pl
from jax.experimental.pallas import tpu as pltpu
from jax.sharding import PartitionSpec as P

WINDOWS = 2
WLEN = 1500
NFREQ = 384
TAPS = 32
MAXLAG = 200
LANES = 128
BLOCKS = -(-WLEN // LANES)
REACH = 3 * LANES
SPAN = 2 * LANES * (BLOCKS - 1) + REACH
PIECES = 2 * NFREQ // LANES
SLOT = 16
HALVES = 2
VMEM_LIMIT = 48 * 1024 * 1024
LOGICAL = pl.DeviceIdType.LOGICAL


def halves(table):
    high = table.astype(jnp.bfloat16)
    return np.stack([high, (table - high.astype(np.float64)).astype(jnp.bfloat16)])


def filter_table():
    k = np.arange(TAPS)
    window = 0.5 - 0.5 * np.cos(2.0 * np.pi * (k + 0.5) / TAPS)
    taps = 0.5 * np.sinc((k - (TAPS - 1) / 2.0) * 0.5) * window
    table = np.zeros((REACH, LANES))
    for n in range(LANES):
        table[2 * n : 2 * n + TAPS, n] = taps
    return halves(table)


def wave_table(times):
    phase = times[:, None] * np.arange(1, NFREQ + 1)[None, :] % WLEN
    angle = 2.0 * np.pi * phase / WLEN
    return np.concatenate([np.cos(angle), -np.sin(angle)], axis=1)


def inverse_table():
    shifts = np.arange(2 * MAXLAG + 1) - MAXLAG
    phase = np.mod(np.arange(1, NFREQ + 1)[:, None] * shifts[None, :], WLEN)
    angle = 2.0 * np.pi * phase / WLEN
    return np.concatenate([np.cos(angle), -np.sin(angle)], axis=0).astype(jnp.bfloat16)


def split_dot(left, right):
    high = left.astype(jnp.bfloat16)
    low = (left - high.astype(jnp.float32)).astype(jnp.bfloat16)
    return jnp.dot(jnp.concatenate([high, low, high], axis=1),
                   jnp.concatenate([right[0], right[0], right[1]], axis=0),
                   preferred_element_type=jnp.float32)


def whiten(spec_re, spec_im):
    power = spec_re * spec_re + spec_im * spec_im
    level = 0.01 * jnp.mean(power, axis=1, keepdims=True)
    factor = 1.0 / jnp.sqrt(power + level + 1e-06)
    return jnp.concatenate([spec_re * factor, spec_im * factor], axis=1)


def kernel(groups, members, *refs):
    operands, out_ref = refs[:5], refs[5]
    held, (padded, lead, blocks, gathered, wide, cross, load_sem, send_sem, recv_sem) = refs[6:11], refs[11:]
    raw_ref, filt_ref, near_ref, far_ref, inv_ref = held
    count = groups * members
    grp, mem = lax.axis_index("grp"), lax.axis_index("mem")
    me = grp * members + mem
    channels, length = raw_ref.shape

    loads = [pltpu.make_async_copy(operands[i], held[i], load_sem.at[i]) for i in range(5)]
    for load in loads[:4]:
        load.start()
    barrier = pltpu.get_barrier_semaphore()

    stride = next(k for k in range(count // 4 + 1, count + 2) if math.gcd(k, count) == 1)

    def peer_of(step):
        return lax.rem(me + step * stride, count)

    def greet(step, carry):
        pl.semaphore_signal(barrier, inc=1, device_id=peer_of(step), device_id_type=LOGICAL)
        return carry

    lax.fori_loop(1, count, greet, 0, unroll=count <= 32)

    whole = length // LANES * LANES
    padded[:, whole:] = jnp.zeros((channels, padded.shape[1] - whole), jnp.float32)
    loads[0].wait()
    padded[:, :length] = raw_ref[...]
    pieces = []
    for w in range(WINDOWS):
        start = 2 * WLEN * w
        base = start // LANES * LANES
        if start == base:
            piece = padded[:, start : start + SPAN]
        else:
            width = SPAN + LANES
            piece = pltpu.roll(padded[:, base : base + width], width - (start - base), 1)
        pieces.append(piece)
        for b in range(BLOCKS):
            row = w * BLOCKS + b
            lead[row : row + 1, :] = piece[:1, 2 * LANES * b : 2 * LANES * b + REACH]

    loads[1].wait()
    first = split_dot(lead[...], filt_ref)
    row = lax.broadcasted_iota(jnp.int32, first.shape, 0)
    beyond = lax.broadcasted_iota(jnp.int32, first.shape, 1) >= WLEN - (BLOCKS - 1) * LANES
    first = jnp.where((lax.rem(row, BLOCKS) == BLOCKS - 1) & beyond, 0.0, first)
    loads[2].wait()
    parts = split_dot(first, near_ref)
    loads[3].wait()
    part_re, part_im = parts[:, :NFREQ], parts[:, NFREQ:]
    turn_re, turn_im = far_ref[:, :NFREQ], far_ref[:, NFREQ:]
    window = lax.broadcasted_iota(jnp.int32, part_re.shape, 0) // BLOCKS
    sums = []
    for turned in (part_re * turn_re - part_im * turn_im, part_re * turn_im + part_im * turn_re):
        sums.append(jnp.concatenate(
            [
                jnp.sum(jnp.where(window == w, turned, 0.0), axis=0, keepdims=True)
                for w in range(WINDOWS)
            ],
            axis=0,
        ))
    white = whiten(*sums)
    gathered[me] = jnp.concatenate(
        [
            white[w : w + 1, LANES * i : LANES * (i + 1)]
            for w in range(WINDOWS)
            for i in range(PIECES)
        ],
        axis=0,
    ).astype(jnp.bfloat16)

    pl.semaphore_wait(barrier, count - 1)

    half = count // HALVES
    mine = me // half

    def send(step, carry):
        pltpu.make_async_remote_copy(
            src_ref=gathered.at[me],
            dst_ref=gathered.at[me],
            send_sem=send_sem,
            recv_sem=recv_sem.at[mine],
            device_id=peer_of(step),
            device_id_type=LOGICAL,
        ).start()
        return carry

    lax.fori_loop(1, count, send, 0, unroll=count <= 32)

    loads[4].start()

    for w in range(WINDOWS):
        for b in range(BLOCKS):
            row = (w * BLOCKS + b) * channels
            blocks[row : row + channels, :] = pieces[w][:, 2 * LANES * b : 2 * LANES * b + REACH]
    decimated = split_dot(blocks[...], filt_ref)
    inside = lax.broadcasted_iota(jnp.int32, (channels, LANES), 1) < WLEN - (BLOCKS - 1) * LANES
    kept = []
    for w in range(WINDOWS):
        first = w * BLOCKS * channels
        last = first + (BLOCKS - 1) * channels
        kept += [decimated[first:last], jnp.where(inside, decimated[last : last + channels], 0.0)]
    decimated = jnp.concatenate(kept, axis=0)

    parts = split_dot(decimated, near_ref)
    sums_re, sums_im = [], []
    for w in range(WINDOWS):
        sum_re = sum_im = None
        for b in range(BLOCKS):
            row = (w * BLOCKS + b) * channels
            part_re = parts[row : row + channels, :NFREQ]
            part_im = parts[row : row + channels, NFREQ:]
            turn_re = far_ref[b : b + 1, :NFREQ]
            turn_im = far_ref[b : b + 1, NFREQ:]
            if b == 0:
                sum_re, sum_im = part_re, part_im
            else:
                sum_re = sum_re + (part_re * turn_re - part_im * turn_im)
                sum_im = sum_im + (part_re * turn_im + part_im * turn_re)
        sums_re.append(sum_re)
        sums_im.append(sum_im)
    spec_re = jnp.concatenate(sums_re, axis=0)
    spec_im = jnp.concatenate(sums_im, axis=0)
    own = whiten(spec_re, spec_im).astype(jnp.bfloat16).astype(jnp.float32)

    panel = min(half, 32)
    scale = 1.0 / math.sqrt(WINDOWS * NFREQ)

    def work(index, carry):
        for j in range(panel):
            wide[j * SLOT : j * SLOT + WINDOWS * PIECES, :] = gathered[index * panel + j].astype(jnp.float32)
        half = PIECES // 2
        for i in range(half):
            real, imag = slice(LANES * i, LANES * (i + 1)), slice(NFREQ + LANES * i, NFREQ + LANES * (i + 1))
            b_re = [wide[pl.ds(w * PIECES + i, panel, stride=SLOT), :] for w in range(WINDOWS)]
            b_im = [wide[pl.ds(w * PIECES + half + i, panel, stride=SLOT), :] for w in range(WINDOWS)]
            for c in range(channels):
                cross_re = cross_im = None
                for w in range(WINDOWS):
                    a_re = own[w * channels + c : w * channels + c + 1, real]
                    a_im = own[w * channels + c : w * channels + c + 1, imag]
                    term_re = a_re * b_re[w] + a_im * b_im[w]
                    term_im = a_im * b_re[w] - a_re * b_im[w]
                    cross_re = term_re if w == 0 else cross_re + term_re
                    cross_im = term_im if w == 0 else cross_im + term_im
                cross[c * panel : (c + 1) * panel, real] = cross_re.astype(jnp.bfloat16)
                cross[c * panel : (c + 1) * panel, imag] = cross_im.astype(jnp.bfloat16)
        corr = jnp.dot(cross[...], inv_ref[...], preferred_element_type=jnp.float32) * scale
        corr = corr.astype(jnp.bfloat16)
        for c in range(channels):
            out_ref[c, pl.ds(pl.multiple_of(index * panel, panel), panel), :] = corr[c * panel : (c + 1) * panel]
        return carry

    loads[4].wait()
    for i in range(HALVES):
        part = mine + i
        part = jnp.where(part >= HALVES, part - HALVES, part)
        arrived = gathered.at[pl.ds(0, half - 1 if i == 0 else half)]
        pltpu.make_async_copy(arrived, arrived, recv_sem.at[part]).wait()
        if half == panel:
            work(part, 0)
        else:
            panels = half // panel
            lax.fori_loop(part * panels, (part + 1) * panels, work, 0)
    others = gathered.at[pl.ds(0, count - 1)]
    pltpu.make_async_copy(others, others, send_sem).wait()


def solution(mesh):
    groups, members = mesh.shape["grp"], mesh.shape["mem"]
    count = groups * members
    tables = [
        filter_table(),
        halves(wave_table(np.arange(LANES))),
        np.tile(wave_table(LANES * np.arange(BLOCKS)), (WINDOWS, 1)).astype(np.float32),
        inverse_table(),
    ]

    def on_device(raw_traces):
        channels, length = raw_traces.shape
        start = 2 * WLEN * (WINDOWS - 1) // LANES * LANES
        operands = [
            pltpu.with_memory_space_constraint(x, pltpu.HBM)
            for x in [raw_traces] + [jnp.asarray(table) for table in tables]
        ]
        return pl.pallas_call(
            functools.partial(kernel, groups, members),
            out_shape=jax.ShapeDtypeStruct((channels, count, 2 * MAXLAG + 1), jnp.bfloat16),
            in_specs=[pl.BlockSpec(memory_space=pl.ANY)] * len(operands),
            out_specs=pl.BlockSpec(memory_space=pltpu.VMEM),
            scratch_shapes=[pltpu.VMEM(x.shape, x.dtype) for x in operands]
            + [
                pltpu.VMEM((channels, start + SPAN + LANES), jnp.float32),
                pltpu.VMEM((WINDOWS * BLOCKS, REACH), jnp.float32),
                pltpu.VMEM((WINDOWS * BLOCKS * channels, REACH), jnp.float32),
                pltpu.VMEM((count, WINDOWS * PIECES, LANES), jnp.bfloat16),
                pltpu.VMEM((min(count // HALVES, 32) * SLOT, LANES), jnp.float32),
                pltpu.VMEM((min(count // HALVES, 32) * channels, 2 * NFREQ), jnp.bfloat16),
                pltpu.SemaphoreType.DMA((len(operands),)),
                pltpu.SemaphoreType.DMA,
                pltpu.SemaphoreType.DMA((HALVES,)),
            ],
            compiler_params=pltpu.CompilerParams(
                collective_id=0, has_side_effects=True, vmem_limit_bytes=VMEM_LIMIT
            ),
        )(*operands)

    return jax.shard_map(
        on_device,
        mesh=mesh,
        in_specs=(P(("grp", "mem"), None),),
        out_specs=P(("grp", "mem"), None, None),
        check_vma=False,
    )
```

```python
import functools
import math

import jax
import jax.numpy as jnp
import numpy as np
from jax import lax
from jax.experimental import pallas as pl
from jax.experimental.pallas import tpu as pltpu
from jax.sharding import PartitionSpec as P

WINDOWS = 2
WLEN = 1500
NFREQ = 384
TAPS = 32
MAXLAG = 200
LANES = 128
BLOCKS = -(-WLEN // LANES)
REACH = 3 * LANES
SPAN = 2 * LANES * (BLOCKS - 1) + REACH
PIECES = 2 * NFREQ // LANES
SLOT = 16
HALVES = 2
VMEM_LIMIT = 48 * 1024 * 1024
LOGICAL = pl.DeviceIdType.LOGICAL


def halves(table):
    high = table.astype(jnp.bfloat16)
    return np.stack([high, (table - high.astype(np.float64)).astype(jnp.bfloat16)])


def filter_table():
    k = np.arange(TAPS)
    window = 0.5 - 0.5 * np.cos(2.0 * np.pi * (k + 0.5) / TAPS)
    taps = 0.5 * np.sinc((k - (TAPS - 1) / 2.0) * 0.5) * window
    table = np.zeros((REACH, LANES))
    for n in range(LANES):
        table[2 * n : 2 * n + TAPS, n] = taps
    return halves(table)


def wave_table(times):
    phase = times[:, None] * np.arange(1, NFREQ + 1)[None, :] % WLEN
    angle = 2.0 * np.pi * phase / WLEN
    return np.concatenate([np.cos(angle), -np.sin(angle)], axis=1)


def inverse_table():
    shifts = np.arange(2 * MAXLAG + 1) - MAXLAG
    phase = np.mod(np.arange(1, NFREQ + 1)[:, None] * shifts[None, :], WLEN)
    angle = 2.0 * np.pi * phase / WLEN
    return np.concatenate([np.cos(angle), -np.sin(angle)], axis=0).astype(jnp.bfloat16)


def split_dot(left, right):
    high = left.astype(jnp.bfloat16)
    low = (left - high.astype(jnp.float32)).astype(jnp.bfloat16)
    return jnp.dot(jnp.concatenate([high, low, high], axis=1),
                   jnp.concatenate([right[0], right[0], right[1]], axis=0),
                   preferred_element_type=jnp.float32)


def whiten(spec_re, spec_im):
    power = spec_re * spec_re + spec_im * spec_im
    level = 0.01 * jnp.mean(power, axis=1, keepdims=True)
    factor = 1.0 / jnp.sqrt(power + level + 1e-06)
    return jnp.concatenate([spec_re * factor, spec_im * factor], axis=1)


def kernel(groups, members, *refs):
    operands, out_ref = refs[:5], refs[5]
    held, (padded, lead, blocks, gathered, wide, cross, load_sem, send_sem, recv_sem) = refs[6:11], refs[11:]
    raw_ref, filt_ref, near_ref, far_ref, inv_ref = held
    count = groups * members
    grp, mem = lax.axis_index("grp"), lax.axis_index("mem")
    me = grp * members + mem
    channels, length = raw_ref.shape

    loads = [pltpu.make_async_copy(operands[i], held[i], load_sem.at[i]) for i in range(5)]
    for load in loads[:4]:
        load.start()
    barrier = pltpu.get_barrier_semaphore()

    bits = range(count.bit_length() - 1)
    flips = [2**b * (1 - 2 * lax.rem(lax.div(me, 2**b), 2)) for b in bits]

    def peer_of(step):
        if count == 2 ** len(bits):
            return me + sum(lax.rem(lax.div(step, 2**b), 2) * flips[b] for b in bits)
        return lax.rem(me + step, count)

    def greet(step, carry):
        pl.semaphore_signal(barrier, inc=1, device_id=peer_of(step), device_id_type=LOGICAL)
        return carry

    lax.fori_loop(1, count, greet, 0, unroll=count <= 32)

    whole = length // LANES * LANES
    padded[:, whole:] = jnp.zeros((channels, padded.shape[1] - whole), jnp.float32)
    loads[0].wait()
    padded[:, :length] = raw_ref[...]
    pieces = []
    for w in range(WINDOWS):
        start = 2 * WLEN * w
        base = start // LANES * LANES
        if start == base:
            piece = padded[:, start : start + SPAN]
        else:
            width = SPAN + LANES
            piece = pltpu.roll(padded[:, base : base + width], width - (start - base), 1)
        pieces.append(piece)
        for b in range(BLOCKS):
            row = w * BLOCKS + b
            lead[row : row + 1, :] = piece[:1, 2 * LANES * b : 2 * LANES * b + REACH]

    loads[1].wait()
    first = split_dot(lead[...], filt_ref)
    row = lax.broadcasted_iota(jnp.int32, first.shape, 0)
    beyond = lax.broadcasted_iota(jnp.int32, first.shape, 1) >= WLEN - (BLOCKS - 1) * LANES
    first = jnp.where((lax.rem(row, BLOCKS) == BLOCKS - 1) & beyond, 0.0, first)
    loads[2].wait()
    parts = split_dot(first, near_ref)
    loads[3].wait()
    part_re, part_im = parts[:, :NFREQ], parts[:, NFREQ:]
    turn_re, turn_im = far_ref[:, :NFREQ], far_ref[:, NFREQ:]
    window = lax.broadcasted_iota(jnp.int32, part_re.shape, 0) // BLOCKS
    sums = []
    for turned in (part_re * turn_re - part_im * turn_im, part_re * turn_im + part_im * turn_re):
        sums.append(jnp.concatenate(
            [
                jnp.sum(jnp.where(window == w, turned, 0.0), axis=0, keepdims=True)
                for w in range(WINDOWS)
            ],
            axis=0,
        ))
    white = whiten(*sums)
    gathered[me] = jnp.concatenate(
        [
            white[w : w + 1, LANES * i : LANES * (i + 1)]
            for w in range(WINDOWS)
            for i in range(PIECES)
        ],
        axis=0,
    ).astype(jnp.bfloat16)

    pl.semaphore_wait(barrier, count - 1)

    half = count // HALVES
    mine = me // half

    def send(step, carry):
        pltpu.make_async_remote_copy(
            src_ref=gathered.at[me],
            dst_ref=gathered.at[me],
            send_sem=send_sem,
            recv_sem=recv_sem.at[mine],
            device_id=peer_of(step),
            device_id_type=LOGICAL,
        ).start()
        return carry

    lax.fori_loop(1, count, send, 0, unroll=count <= 32)

    loads[4].start()

    for w in range(WINDOWS):
        for b in range(BLOCKS):
            row = (w * BLOCKS + b) * channels
            blocks[row : row + channels, :] = pieces[w][:, 2 * LANES * b : 2 * LANES * b + REACH]
    decimated = split_dot(blocks[...], filt_ref)
    inside = lax.broadcasted_iota(jnp.int32, (channels, LANES), 1) < WLEN - (BLOCKS - 1) * LANES
    kept = []
    for w in range(WINDOWS):
        first = w * BLOCKS * channels
        last = first + (BLOCKS - 1) * channels
        kept += [decimated[first:last], jnp.where(inside, decimated[last : last + channels], 0.0)]
    decimated = jnp.concatenate(kept, axis=0)

    parts = split_dot(decimated, near_ref)
    sums_re, sums_im = [], []
    for w in range(WINDOWS):
        sum_re = sum_im = None
        for b in range(BLOCKS):
            row = (w * BLOCKS + b) * channels
            part_re = parts[row : row + channels, :NFREQ]
            part_im = parts[row : row + channels, NFREQ:]
            turn_re = far_ref[b : b + 1, :NFREQ]
            turn_im = far_ref[b : b + 1, NFREQ:]
            if b == 0:
                sum_re, sum_im = part_re, part_im
            else:
                sum_re = sum_re + (part_re * turn_re - part_im * turn_im)
                sum_im = sum_im + (part_re * turn_im + part_im * turn_re)
        sums_re.append(sum_re)
        sums_im.append(sum_im)
    spec_re = jnp.concatenate(sums_re, axis=0)
    spec_im = jnp.concatenate(sums_im, axis=0)
    own = whiten(spec_re, spec_im).astype(jnp.bfloat16).astype(jnp.float32)

    panel = min(half, 32)
    scale = 1.0 / math.sqrt(WINDOWS * NFREQ)

    def work(index, carry):
        for j in range(panel):
            wide[j * SLOT : j * SLOT + WINDOWS * PIECES, :] = gathered[index * panel + j].astype(jnp.float32)
        half = PIECES // 2
        for i in range(half):
            real, imag = slice(LANES * i, LANES * (i + 1)), slice(NFREQ + LANES * i, NFREQ + LANES * (i + 1))
            b_re = [wide[pl.ds(w * PIECES + i, panel, stride=SLOT), :] for w in range(WINDOWS)]
            b_im = [wide[pl.ds(w * PIECES + half + i, panel, stride=SLOT), :] for w in range(WINDOWS)]
            for c in range(channels):
                cross_re = cross_im = None
                for w in range(WINDOWS):
                    a_re = own[w * channels + c : w * channels + c + 1, real]
                    a_im = own[w * channels + c : w * channels + c + 1, imag]
                    term_re = a_re * b_re[w] + a_im * b_im[w]
                    term_im = a_im * b_re[w] - a_re * b_im[w]
                    cross_re = term_re if w == 0 else cross_re + term_re
                    cross_im = term_im if w == 0 else cross_im + term_im
                cross[c * panel : (c + 1) * panel, real] = cross_re.astype(jnp.bfloat16)
                cross[c * panel : (c + 1) * panel, imag] = cross_im.astype(jnp.bfloat16)
        corr = jnp.dot(cross[...], inv_ref[...], preferred_element_type=jnp.float32) * scale
        corr = corr.astype(jnp.bfloat16)
        for c in range(channels):
            out_ref[c, pl.ds(pl.multiple_of(index * panel, panel), panel), :] = corr[c * panel : (c + 1) * panel]
        return carry

    loads[4].wait()
    for i in range(HALVES):
        part = mine + i
        part = jnp.where(part >= HALVES, part - HALVES, part)
        arrived = gathered.at[pl.ds(0, half - 1 if i == 0 else half)]
        pltpu.make_async_copy(arrived, arrived, recv_sem.at[part]).wait()
        if half == panel:
            work(part, 0)
        else:
            panels = half // panel
            lax.fori_loop(part * panels, (part + 1) * panels, work, 0)
    others = gathered.at[pl.ds(0, count - 1)]
    pltpu.make_async_copy(others, others, send_sem).wait()


def solution(mesh):
    groups, members = mesh.shape["grp"], mesh.shape["mem"]
    count = groups * members
    tables = [
        filter_table(),
        halves(wave_table(np.arange(LANES))),
        np.tile(wave_table(LANES * np.arange(BLOCKS)), (WINDOWS, 1)).astype(np.float32),
        inverse_table(),
    ]

    def on_device(raw_traces):
        channels, length = raw_traces.shape
        start = 2 * WLEN * (WINDOWS - 1) // LANES * LANES
        operands = [
            pltpu.with_memory_space_constraint(x, pltpu.HBM)
            for x in [raw_traces] + [jnp.asarray(table) for table in tables]
        ]
        return pl.pallas_call(
            functools.partial(kernel, groups, members),
            out_shape=jax.ShapeDtypeStruct((channels, count, 2 * MAXLAG + 1), jnp.bfloat16),
            in_specs=[pl.BlockSpec(memory_space=pl.ANY)] * len(operands),
            out_specs=pl.BlockSpec(memory_space=pltpu.VMEM),
            scratch_shapes=[pltpu.VMEM(x.shape, x.dtype) for x in operands]
            + [
                pltpu.VMEM((channels, start + SPAN + LANES), jnp.float32),
                pltpu.VMEM((WINDOWS * BLOCKS, REACH), jnp.float32),
                pltpu.VMEM((WINDOWS * BLOCKS * channels, REACH), jnp.float32),
                pltpu.VMEM((count, WINDOWS * PIECES, LANES), jnp.bfloat16),
                pltpu.VMEM((min(count // HALVES, 32) * SLOT, LANES), jnp.float32),
                pltpu.VMEM((min(count // HALVES, 32) * channels, 2 * NFREQ), jnp.bfloat16),
                pltpu.SemaphoreType.DMA((len(operands),)),
                pltpu.SemaphoreType.DMA,
                pltpu.SemaphoreType.DMA((HALVES,)),
            ],
            compiler_params=pltpu.CompilerParams(
                collective_id=0, has_side_effects=True, vmem_limit_bytes=VMEM_LIMIT
            ),
        )(*operands)

    return jax.shard_map(
        on_device,
        mesh=mesh,
        in_specs=(P(("grp", "mem"), None),),
        out_specs=P(("grp", "mem"), None, None),
        check_vma=False,
    )
```

```python
import functools
import math

import jax
import jax.numpy as jnp
import numpy as np
from jax import lax
from jax.experimental import pallas as pl
from jax.experimental.pallas import tpu as pltpu
from jax.sharding import PartitionSpec as P

WINDOWS = 2
WLEN = 1500
NFREQ = 384
TAPS = 32
MAXLAG = 200
LANES = 128
BLOCKS = -(-WLEN // LANES)
REACH = 3 * LANES
SPAN = 2 * LANES * (BLOCKS - 1) + REACH
PIECES = 2 * NFREQ // LANES
SLOT = 16
HALVES = 2
VMEM_LIMIT = 48 * 1024 * 1024
LOGICAL = pl.DeviceIdType.LOGICAL


def halves(table):
    high = table.astype(jnp.bfloat16)
    return np.stack([high, (table - high.astype(np.float64)).astype(jnp.bfloat16)])


def filter_table():
    k = np.arange(TAPS)
    window = 0.5 - 0.5 * np.cos(2.0 * np.pi * (k + 0.5) / TAPS)
    taps = 0.5 * np.sinc((k - (TAPS - 1) / 2.0) * 0.5) * window
    table = np.zeros((REACH, LANES))
    for n in range(LANES):
        table[2 * n : 2 * n + TAPS, n] = taps
    return halves(table)


def wave_table(times):
    phase = times[:, None] * np.arange(1, NFREQ + 1)[None, :] % WLEN
    angle = 2.0 * np.pi * phase / WLEN
    return np.concatenate([np.cos(angle), -np.sin(angle)], axis=1)


def inverse_table():
    shifts = np.arange(2 * MAXLAG + 1) - MAXLAG
    phase = np.mod(np.arange(1, NFREQ + 1)[:, None] * shifts[None, :], WLEN)
    angle = 2.0 * np.pi * phase / WLEN
    return np.concatenate([np.cos(angle), -np.sin(angle)], axis=0).astype(jnp.bfloat16)


def split_dot(left, right):
    high = left.astype(jnp.bfloat16)
    low = (left - high.astype(jnp.float32)).astype(jnp.bfloat16)
    return jnp.dot(jnp.concatenate([high, low, high], axis=1),
                   jnp.concatenate([right[0], right[0], right[1]], axis=0),
                   preferred_element_type=jnp.float32)


def whiten(spec_re, spec_im):
    power = spec_re * spec_re + spec_im * spec_im
    level = 0.01 * jnp.mean(power, axis=1, keepdims=True)
    factor = 1.0 / jnp.sqrt(power + level + 1e-06)
    return jnp.concatenate([spec_re * factor, spec_im * factor], axis=1)


def kernel(groups, members, *refs):
    operands, out_ref = refs[:5], refs[5]
    held, (padded, lead, blocks, gathered, wide, cross, load_sem, send_sem, recv_sem) = refs[6:11], refs[11:]
    raw_ref, filt_ref, near_ref, far_ref, inv_ref = held
    count = groups * members
    grp, mem = lax.axis_index("grp"), lax.axis_index("mem")
    me = grp * members + mem
    channels, length = raw_ref.shape

    loads = [pltpu.make_async_copy(operands[i], held[i], load_sem.at[i]) for i in range(5)]
    for load in loads[:4]:
        load.start()
    barrier = pltpu.get_barrier_semaphore()

    def peer_of(step):
        peer = me - step
        return jnp.where(peer < 0, peer + count, peer)

    def greet(step, carry):
        pl.semaphore_signal(barrier, inc=1, device_id=peer_of(step), device_id_type=LOGICAL)
        return carry

    lax.fori_loop(1, count, greet, 0, unroll=count <= 32)

    whole = length // LANES * LANES
    padded[:, whole:] = jnp.zeros((channels, padded.shape[1] - whole), jnp.float32)
    loads[0].wait()
    padded[:, :length] = raw_ref[...]
    pieces = []
    for w in range(WINDOWS):
        start = 2 * WLEN * w
        base = start // LANES * LANES
        if start == base:
            piece = padded[:, start : start + SPAN]
        else:
            width = SPAN + LANES
            piece = pltpu.roll(padded[:, base : base + width], width - (start - base), 1)
        pieces.append(piece)
        for b in range(BLOCKS):
            row = w * BLOCKS + b
            lead[row : row + 1, :] = piece[:1, 2 * LANES * b : 2 * LANES * b + REACH]

    loads[1].wait()
    first = split_dot(lead[...], filt_ref)
    row = lax.broadcasted_iota(jnp.int32, first.shape, 0)
    beyond = lax.broadcasted_iota(jnp.int32, first.shape, 1) >= WLEN - (BLOCKS - 1) * LANES
    first = jnp.where((lax.rem(row, BLOCKS) == BLOCKS - 1) & beyond, 0.0, first)
    loads[2].wait()
    parts = split_dot(first, near_ref)
    loads[3].wait()
    part_re, part_im = parts[:, :NFREQ], parts[:, NFREQ:]
    turn_re, turn_im = far_ref[:, :NFREQ], far_ref[:, NFREQ:]
    window = lax.broadcasted_iota(jnp.int32, part_re.shape, 0) // BLOCKS
    sums = []
    for turned in (part_re * turn_re - part_im * turn_im, part_re * turn_im + part_im * turn_re):
        sums.append(jnp.concatenate(
            [
                jnp.sum(jnp.where(window == w, turned, 0.0), axis=0, keepdims=True)
                for w in range(WINDOWS)
            ],
            axis=0,
        ))
    white = whiten(*sums)
    gathered[me] = jnp.concatenate(
        [
            white[w : w + 1, LANES * i : LANES * (i + 1)]
            for w in range(WINDOWS)
            for i in range(PIECES)
        ],
        axis=0,
    ).astype(jnp.bfloat16)

    pl.semaphore_wait(barrier, count - 1)

    half = count // HALVES
    mine = me // half

    def send(step, carry):
        pltpu.make_async_remote_copy(
            src_ref=gathered.at[me],
            dst_ref=gathered.at[me],
            send_sem=send_sem,
            recv_sem=recv_sem.at[mine],
            device_id=peer_of(step),
            device_id_type=LOGICAL,
        ).start()
        return carry

    lax.fori_loop(1, count, send, 0, unroll=count <= 32)

    loads[4].start()

    for w in range(WINDOWS):
        for b in range(BLOCKS):
            row = (w * BLOCKS + b) * channels
            blocks[row : row + channels, :] = pieces[w][:, 2 * LANES * b : 2 * LANES * b + REACH]
    decimated = split_dot(blocks[...], filt_ref)
    inside = lax.broadcasted_iota(jnp.int32, (channels, LANES), 1) < WLEN - (BLOCKS - 1) * LANES
    kept = []
    for w in range(WINDOWS):
        first = w * BLOCKS * channels
        last = first + (BLOCKS - 1) * channels
        kept += [decimated[first:last], jnp.where(inside, decimated[last : last + channels], 0.0)]
    decimated = jnp.concatenate(kept, axis=0)

    parts = split_dot(decimated, near_ref)
    sums_re, sums_im = [], []
    for w in range(WINDOWS):
        sum_re = sum_im = None
        for b in range(BLOCKS):
            row = (w * BLOCKS + b) * channels
            part_re = parts[row : row + channels, :NFREQ]
            part_im = parts[row : row + channels, NFREQ:]
            turn_re = far_ref[b : b + 1, :NFREQ]
            turn_im = far_ref[b : b + 1, NFREQ:]
            if b == 0:
                sum_re, sum_im = part_re, part_im
            else:
                sum_re = sum_re + (part_re * turn_re - part_im * turn_im)
                sum_im = sum_im + (part_re * turn_im + part_im * turn_re)
        sums_re.append(sum_re)
        sums_im.append(sum_im)
    spec_re = jnp.concatenate(sums_re, axis=0)
    spec_im = jnp.concatenate(sums_im, axis=0)
    own = whiten(spec_re, spec_im).astype(jnp.bfloat16).astype(jnp.float32)

    panel = min(half, 32)
    scale = 1.0 / math.sqrt(WINDOWS * NFREQ)

    def work(index, carry):
        for j in range(panel):
            wide[j * SLOT : j * SLOT + WINDOWS * PIECES, :] = gathered[index * panel + j].astype(jnp.float32)
        half = PIECES // 2
        for i in range(half):
            real, imag = slice(LANES * i, LANES * (i + 1)), slice(NFREQ + LANES * i, NFREQ + LANES * (i + 1))
            b_re = [wide[pl.ds(w * PIECES + i, panel, stride=SLOT), :] for w in range(WINDOWS)]
            b_im = [wide[pl.ds(w * PIECES + half + i, panel, stride=SLOT), :] for w in range(WINDOWS)]
            for c in range(channels):
                cross_re = cross_im = None
                for w in range(WINDOWS):
                    a_re = own[w * channels + c : w * channels + c + 1, real]
                    a_im = own[w * channels + c : w * channels + c + 1, imag]
                    term_re = a_re * b_re[w] + a_im * b_im[w]
                    term_im = a_im * b_re[w] - a_re * b_im[w]
                    cross_re = term_re if w == 0 else cross_re + term_re
                    cross_im = term_im if w == 0 else cross_im + term_im
                cross[c * panel : (c + 1) * panel, real] = cross_re.astype(jnp.bfloat16)
                cross[c * panel : (c + 1) * panel, imag] = cross_im.astype(jnp.bfloat16)
        corr = jnp.dot(cross[...], inv_ref[...], preferred_element_type=jnp.float32) * scale
        corr = corr.astype(jnp.bfloat16)
        for c in range(channels):
            out_ref[c, pl.ds(pl.multiple_of(index * panel, panel), panel), :] = corr[c * panel : (c + 1) * panel]
        return carry

    loads[4].wait()
    for i in range(HALVES):
        part = mine + i
        part = jnp.where(part >= HALVES, part - HALVES, part)
        arrived = gathered.at[pl.ds(0, half - 1 if i == 0 else half)]
        pltpu.make_async_copy(arrived, arrived, recv_sem.at[part]).wait()
        if half == panel:
            work(part, 0)
        else:
            panels = half // panel
            lax.fori_loop(part * panels, (part + 1) * panels, work, 0)
    others = gathered.at[pl.ds(0, count - 1)]
    pltpu.make_async_copy(others, others, send_sem).wait()


def solution(mesh):
    groups, members = mesh.shape["grp"], mesh.shape["mem"]
    count = groups * members
    tables = [
        filter_table(),
        halves(wave_table(np.arange(LANES))),
        np.tile(wave_table(LANES * np.arange(BLOCKS)), (WINDOWS, 1)).astype(np.float32),
        inverse_table(),
    ]

    def on_device(raw_traces):
        channels, length = raw_traces.shape
        start = 2 * WLEN * (WINDOWS - 1) // LANES * LANES
        operands = [
            pltpu.with_memory_space_constraint(x, pltpu.HBM)
            for x in [raw_traces] + [jnp.asarray(table) for table in tables]
        ]
        return pl.pallas_call(
            functools.partial(kernel, groups, members),
            out_shape=jax.ShapeDtypeStruct((channels, count, 2 * MAXLAG + 1), jnp.bfloat16),
            in_specs=[pl.BlockSpec(memory_space=pl.ANY)] * len(operands),
            out_specs=pl.BlockSpec(memory_space=pltpu.VMEM),
            scratch_shapes=[pltpu.VMEM(x.shape, x.dtype) for x in operands]
            + [
                pltpu.VMEM((channels, start + SPAN + LANES), jnp.float32),
                pltpu.VMEM((WINDOWS * BLOCKS, REACH), jnp.float32),
                pltpu.VMEM((WINDOWS * BLOCKS * channels, REACH), jnp.float32),
                pltpu.VMEM((count, WINDOWS * PIECES, LANES), jnp.bfloat16),
                pltpu.VMEM((min(count // HALVES, 32) * SLOT, LANES), jnp.float32),
                pltpu.VMEM((min(count // HALVES, 32) * channels, 2 * NFREQ), jnp.bfloat16),
                pltpu.SemaphoreType.DMA((len(operands),)),
                pltpu.SemaphoreType.DMA,
                pltpu.SemaphoreType.DMA((HALVES,)),
            ],
            compiler_params=pltpu.CompilerParams(
                collective_id=0, has_side_effects=True, vmem_limit_bytes=VMEM_LIMIT
            ),
        )(*operands)

    return jax.shard_map(
        on_device,
        mesh=mesh,
        in_specs=(P(("grp", "mem"), None),),
        out_specs=P(("grp", "mem"), None, None),
        check_vma=False,
    )
```
